128 devices in a mesh: dp: 16 (over x, z), enc: 8 (over y, core).
Axes of the slice: x: 4, y: 4, z: 4, core: 2. Of those that a mesh axis runs over, the one named last changes fastest.
Arguments:
- tokens: bfloat16 [4096, 4096], P('dp'), may hold values from -10 to 10
- store: bfloat16 [1024, 128, 4096], P(('dp', 'enc')), may hold values from -10 to 10
- holder: int32 [128, 1], P('dp'), may hold values from 0 to 7; in each aligned block of 8 rows (0 to 7, 8 to 15, ...) at most 3 rows name the same one
- rows: int32 [128], P('dp'), may hold values from 0 to 7
- wq: bfloat16 [4096, 2048], P('dp', 'enc'), may hold values from -0.1015625 to 0.1015625
- wk: bfloat16 [4096, 2048], P('dp', 'enc'), may hold values from -0.1015625 to 0.1015625
- wv: bfloat16 [4096, 2048], P('dp', 'enc'), may hold values from -0.09375 to 0.09375
- wo: bfloat16 [2048, 4096], P('enc', 'dp'), may hold values from -0.125 to 0.125
- cotangent: bfloat16 [4096, 4096], P('dp'), may hold values from -6 to 6
Outputs:
- cca_out: bfloat16 [4096, 4096], P('dp', 'enc')
- grad_tokens: bfloat16 [4096, 4096], P('dp', 'enc')
- grad_wq: bfloat16 [4096, 2048], P('dp', 'enc')
- grad_wk: bfloat16 [4096, 2048], P('dp', 'enc')
- grad_wv: bfloat16 [4096, 2048], P('dp', 'enc')
- grad_wo: bfloat16 [2048, 4096], P('enc', 'dp')
The draws below stay inside these ranges and needn't reach their ends.
Inputs may be any that keep to these rules, and one draw needn't show every extreme that they name: `holder`: in each aligned block of 8 entries (the neighbours of one dp index) no enc index appears more than 3 times; in some blocks one appears exactly 3 times.
All inputs are finite; a program needn't handle non-finite values.
Results may differ from the reference program's by a relative error of at most 0.024.
The reference program's roundings to bfloat16 on the way count: a program that leaves them out, or rounds other values in their place, can miss the bound.
Values may be sent and summed in bfloat16 or wider, within the bound.
A program may use at most 128 MiB of HBM per device.

```python
import math
import jax
import jax.numpy as jnp
import numpy as np
from jax import lax

D = 4096
HEADS = 16
HD = 128
CL = 64
NLEN = 128
CAP = 3
SPANS_DP = 4
NB_DEV = 8
HW = 2048
TOK_DP = 256
TOKENS = 4096
NEIGH_DP = 8
NEIGHBOURS = 128
ENC_ROWS = 1024
N_DP = 16
N_ENC = 8


def draw_tokens(key, part):
    key = jax.random.fold_in(key, 11)
    first = jax.random.fold_in(key, 0)
    base = jnp.clip(jax.random.normal(first, (TOKENS, D), jnp.float32), -6.0, 6.0)
    return base.astype(jnp.bfloat16)


def draw_store(key, part):
    key = jax.random.fold_in(key, 12)
    first = jax.random.fold_in(key, 0)
    base = jnp.clip(jax.random.normal(first, (ENC_ROWS, NLEN, D), jnp.float32), -6.0, 6.0)
    return base.astype(jnp.bfloat16)


def projection(key):
    base = jnp.clip(jax.random.normal(key, (D, HW), jnp.float32), -5.8, 5.8) / D ** 0.5
    return base.astype(jnp.bfloat16)


def draw_wq(key, part):
    key = jax.random.fold_in(key, 13)
    return projection(key)


def draw_wk(key, part):
    key = jax.random.fold_in(key, 14)
    return projection(key)


def set_ends(array, stream_key, least, largest):
    longest = array.shape.index(max(array.shape))
    spots = []
    for shift in (0, 1):
        where = [jax.random.randint(jax.random.fold_in(stream_key, axis), (), 0, length) for axis, length in enumerate(array.shape)]
        where[longest] = (where[longest] + shift) % array.shape[longest]
        spots.append(tuple(where))
    return array.at[spots[0]].set(least).at[spots[1]].set(largest)


def shard_levels(stream_key, dims, pieces, least, largest):
    level = 1.0
    for position, shards_of in pieces:
        steps = jax.random.uniform(jax.random.fold_in(jax.random.fold_in(stream_key, 6), position), (shards_of,), jnp.float32, least / len(pieces), largest / len(pieces))
        level = level * jnp.repeat(jnp.exp(steps), dims[position] // shards_of).reshape((-1,) + (1,) * (len(dims) - 1 - position))
    return level


def routed_block(rng, own, number, rows, count, top, bound, skew):
    ranking = jax.random.permutation(rng, count)
    heavy_load, common = portions_of(count, rows * top, bound, skew, True), portions_of(count, rows * top, bound, skew, False)
    places = jnp.arange(count)

    def named(lengths, turn):
        used = int((lengths > 0).sum())
        fixed = max(1, used // 4)
        moved = fixed + (places - fixed + turn * (used - fixed)) % max(1, count - fixed)
        return jnp.zeros((count,), jnp.int32).at[ranking[jnp.where(places < fixed, places, moved)]].set(jnp.asarray(lengths, jnp.int32))

    lengths = jnp.where(number % 4 == 0, named(heavy_load, number // 4), named(common, number - number // 4 - 1))
    mixed = jax.random.permutation(jax.random.fold_in(own, 3), count)
    source_of, receiver = mixed[0:count // 2 * 2:2], mixed[1:count // 2 * 2:2]
    room = jnp.minimum(lengths[source_of] - 1, bound - lengths[receiver]) // 2
    room = jnp.where((source_of == ranking[0]) | (receiver == ranking[0]) | (lengths[receiver] == 0), 0, jnp.maximum(room, 0))
    moved = jax.random.randint(jax.random.fold_in(own, 4), (count // 2,), 0, 1 << 20) % (room + 1)
    lengths = lengths.at[source_of].add(-moved).at[receiver].add(moved)
    items = jnp.searchsorted(jnp.cumsum(lengths), jnp.arange(rows * top), side="right").astype(jnp.int32)
    listing = items.reshape(top, rows).T
    listing = listing[jax.random.permutation(jax.random.fold_in(own, 1), rows)]
    turn = jax.random.randint(jax.random.fold_in(own, 2), (rows, 1), 0, top)
    return jnp.take_along_axis(listing, (jnp.arange(top)[None, :] + turn) % top, axis=1)


def portions_of(amount, total, bound, skew, full):
    loads = [(1 << 20) // math.isqrt(standing ** skew) + 1 for standing in range(1, amount + 1)]
    largest = bound if full else min(bound, max(-(-total // amount), total * loads[0] // sum(loads)))
    least = 1 if total - largest >= amount - 1 else 0
    given, spare = [largest] + [least] * (amount - 1), total - largest - least * (amount - 1)
    while spare > 0:
        free = [i for i in range(1, amount) if given[i] < largest] or [i for i in range(1, amount) if given[i] < bound]
        mass, remaining = sum([loads[i] for i in free]), spare
        for i in free:
            more = min(bound - given[i], max(1, remaining * loads[i] // mass), spare)
            given[i] = given[i] + more
            spare = spare - more
    return np.array(given)


def centred(rng, extent, deviation, limit, pieces=(), kind=jnp.bfloat16):
    entries = jax.random.normal(rng, extent, jnp.float32) * deviation
    if len(pieces) > 0:
        entries = shard_levels(rng, extent, pieces, -0.22, 0.18) * entries
    return jnp.clip(entries, min=-limit, max=limit).astype(kind)


def setup_inputs(seed: int = 0) -> dict:
    splits = jax.random.split(jax.random.key(seed), 10)
    tokens = draw_tokens(jax.random.fold_in(splits[9], 71), 0)
    store = draw_store(jax.random.fold_in(splits[9], 71), 0)
    holder_keys = jax.random.split(jax.random.fold_in(splits[2], 1), NEIGHBOURS // NEIGH_DP)
    holder_turns = jax.random.permutation(jax.random.fold_in(splits[2], 3), NEIGHBOURS // NEIGH_DP)
    holder = jax.vmap(lambda own, number: routed_block(jax.random.fold_in(splits[2], 2), own, number, NEIGH_DP, N_ENC, 1, CAP, 2))(holder_keys, holder_turns).reshape((NEIGHBOURS, 1))
    rows = set_ends(jax.random.randint(splits[3], (NEIGHBOURS,), 0, NB_DEV), jax.random.fold_in(splits[3], 1), 0, NB_DEV - 1).astype(jnp.int32)
    wq = draw_wq(jax.random.fold_in(splits[9], 71), 0)
    wk = draw_wk(jax.random.fold_in(splits[9], 71), 0)
    wv = centred(splits[6], (D, HW), D ** -0.5, 0.09375, ((0, 16), (1, 8)))
    wo = centred(splits[7], (HW, D), HW ** -0.5, 0.125, ((0, 8), (1, 16)))
    cotangent = centred(splits[8], (TOKENS, D), 1.0, 6.0, ((0, 16),))
    return dict(tokens=tokens, store=store, holder=holder, rows=rows, wq=wq, wk=wk, wv=wv, wo=wo, cotangent=cotangent)


def held(x):
    return lax.optimization_barrier(x.astype(jnp.bfloat16)).astype(jnp.float32)

def settle(terms):
    return lax.optimization_barrier(jnp.sum(held(terms), axis=0)).astype(jnp.bfloat16)

def group_pass(x, grad_out, flat, wq, wk, wv, wo):
    scale = 1.0 / math.sqrt(HD)
    width = HW // N_ENC
    query = jnp.dot(x, wq, preferred_element_type=jnp.float32).astype(jnp.bfloat16)
    keys = jnp.dot(flat, wk, preferred_element_type=jnp.float32).astype(jnp.bfloat16)
    values = jnp.dot(flat, wv, preferred_element_type=jnp.float32).astype(jnp.bfloat16)
    qf = query.astype(jnp.float32).reshape(SPANS_DP, CL, HEADS, HD)
    kf = keys.astype(jnp.float32).reshape(SPANS_DP, 2 * NLEN, HEADS, HD)
    vf = values.astype(jnp.float32).reshape(SPANS_DP, 2 * NLEN, HEADS, HD)
    scores = jnp.einsum('cqhe,ckhe->chqk', qf, kf) * scale
    probs = jax.nn.softmax(scores, axis=-1)
    pbf = held(probs)
    mixed = jnp.einsum('chqk,ckhe->cqhe', pbf, vf).astype(jnp.bfloat16).reshape(TOK_DP, HW)
    out_terms = jnp.einsum('tgj,gjd->gtd', mixed.astype(jnp.float32).reshape(TOK_DP, N_ENC, width), wo.astype(jnp.float32).reshape(N_ENC, width, D))
    cca = settle(out_terms)
    d_mixed = jnp.dot(grad_out, wo.T, preferred_element_type=jnp.float32).astype(jnp.bfloat16)
    grad_wo = jnp.dot(mixed.T, grad_out, preferred_element_type=jnp.float32).astype(jnp.bfloat16)
    dmf = d_mixed.astype(jnp.float32).reshape(SPANS_DP, CL, HEADS, HD)
    dprob = jnp.einsum('cqhe,ckhe->chqk', dmf, vf)
    dscore = probs * (dprob - lax.optimization_barrier(jnp.sum(dprob * probs, axis=-1, keepdims=True))) * scale
    dsf = held(dscore)
    d_query = jnp.einsum('chqk,ckhe->cqhe', dsf, kf).astype(jnp.bfloat16).reshape(TOK_DP, HW)
    d_keys = jnp.einsum('chqk,cqhe->ckhe', dsf, qf).astype(jnp.bfloat16).reshape(NEIGH_DP * NLEN, HW)
    d_values = jnp.einsum('chqk,cqhe->ckhe', pbf, dmf).astype(jnp.bfloat16).reshape(NEIGH_DP * NLEN, HW)
    grad_wq = jnp.dot(x.T, d_query, preferred_element_type=jnp.float32).astype(jnp.bfloat16)
    grad_wk = jnp.dot(flat.T, d_keys, preferred_element_type=jnp.float32).astype(jnp.bfloat16)
    grad_wv = jnp.dot(flat.T, d_values, preferred_element_type=jnp.float32).astype(jnp.bfloat16)
    input_terms = jnp.einsum('tgj,dgj->gtd', d_query.astype(jnp.float32).reshape(TOK_DP, N_ENC, width), wq.astype(jnp.float32).reshape(D, N_ENC, width))
    grad_x = settle(input_terms)
    return (cca, grad_x, grad_wq, grad_wk, grad_wv, grad_wo)

def reference(tokens, store, holder, rows, wq, wk, wv, wo, cotangent):
    group = (jnp.arange(NEIGHBOURS, dtype=jnp.int32) // NEIGH_DP).astype(jnp.int32)
    index = ((group * N_ENC + holder[:, 0]) * NB_DEV + rows).astype(jnp.int32)
    xs = (tokens.reshape(N_DP, TOK_DP, D), cotangent.reshape(N_DP, TOK_DP, D), index.reshape(N_DP, NEIGH_DP))

    def step(carry, item):
        x, grad_out, picks = item
        flat = jnp.take(store, picks, axis=0).reshape(NEIGH_DP * NLEN, D)
        cca, grad_x, gq, gk, gv, go = group_pass(x, grad_out, flat, wq, wk, wv, wo)
        carry = (carry[0] + gq.astype(jnp.float32), carry[1] + gk.astype(jnp.float32), carry[2] + gv.astype(jnp.float32), carry[3] + go.astype(jnp.float32))
        return (carry, (cca, grad_x))
    start = (jnp.zeros((D, HW), jnp.float32), jnp.zeros((D, HW), jnp.float32), jnp.zeros((D, HW), jnp.float32), jnp.zeros((HW, D), jnp.float32))
    sums, (cca, grad_x) = lax.scan(step, start, xs)
    return (cca.reshape(TOKENS, D), grad_x.reshape(TOKENS, D), sums[0].astype(jnp.bfloat16), sums[1].astype(jnp.bfloat16), sums[2].astype(jnp.bfloat16), sums[3].astype(jnp.bfloat16))
```

```python
import functools
import math

import jax
import jax.numpy as jnp
from jax import lax
from jax.experimental import pallas as pl
from jax.experimental.pallas import tpu as pltpu
from jax.sharding import PartitionSpec as P

ANY = pl.BlockSpec(memory_space=pl.ANY)
VMEM = pl.BlockSpec(memory_space=pltpu.VMEM)
SMEM = pl.BlockSpec(memory_space=pltpu.SMEM)
CAP = 3
STEPS = 9
TREES = 8
SEMS = 20
HD = 128


def place():
    dp = lax.axis_index("dp")
    enc = lax.axis_index("enc")
    return dp // 4, dp % 4, enc // 2, enc % 2


def around(value, by):
    return lax.rem(value + (4 + by), 4)


def remote(src, dst, send, recv, target):
    return pltpu.make_async_remote_copy(
        src_ref=src, dst_ref=dst, send_sem=send, recv_sem=recv,
        device_id=target, device_id_type=pl.DeviceIdType.MESH,
    )


def greet(peers):
    barrier = pltpu.get_barrier_semaphore()
    for peer in peers:
        pl.semaphore_signal(barrier, inc=1, device_id=peer, device_id_type=pl.DeviceIdType.MESH)
    pl.semaphore_wait(barrier, len(peers))


def gather_kernel(table, wq, wk, wv, wo, picked, weights, pool,
                  own, got, staged, tree_send, tree_recv, keep_sem,
                  ring_send, ring_recv, save_sem, pair_send, pair_recv):
    x, z, y, core = place()
    dp = x * 4 + z
    sources = (wk, wv, wq, wo)
    spots = (1, 2, 0, 3)

    def dp_at(axis, by):
        if axis == 0:
            return around(x, by) * 4 + z
        return x * 4 + around(z, by)

    def dp_of(first, o1, o2):
        if first == 0:
            return around(x, o1) * 4 + around(z, o2)
        return around(x, o2) * 4 + around(z, o1)

    def enc_at(by):
        return around(y, by) * 2 + core

    sibling = {"enc": y * 2 + 1 - core}
    greet([{"dp": dp_at(a, b)} for a in (0, 1) for b in (1, -1)]
          + [{"enc": enc_at(1)}, {"enc": enc_at(-1)}, sibling])

    sends = []

    def go(copy):
        copy.start()
        sends.append(copy)

    half = 128
    quarter = half // 2
    keeps = []
    for i in range(4):
        copy = pltpu.make_async_copy(sources[i], weights.at[spots[i], dp], keep_sem.at[i])
        copy.start()
        keeps.append(copy)

    def slot(t, j, part=None):
        w = t // 2
        r0 = (t % 2) * half
        if part is None:
            return weights.at[spots[w], j, pl.ds(r0, half)]
        return weights.at[spots[w], j, pl.ds(r0 + part * quarter, quarter)]

    def sem(t, k):
        return tree_send.at[t * SEMS + k], tree_recv.at[t * SEMS + k]

    def push(t, k, src, dst, axis, by):
        s, r = sem(t, k)
        go(remote(src, dst, s, r, {"dp": dp_at(axis, by)}))

    def landed(t, k, dst, axis, by):
        s, r = sem(t, k)
        remote(dst, dst, s, r, {"dp": dp_at(axis, by)}).wait_recv()

    def own_half(t):
        return sources[t // 2].at[pl.ds((t % 2) * half, half)]

    offsets = (0, -1, 1, 2)

    def tree_events(t):
        first = t % 2
        second = 1 - first
        me = dp

        def e0():
            push(t, 0, own_half(t), slot(t, me), first, 1)
            push(t, 1, own_half(t), slot(t, me), first, -1)

        def e0b():
            push(t, 4, own_half(t), slot(t, me), second, 1)
            push(t, 8, own_half(t), slot(t, me), second, -1)

        def e1():
            j = dp_of(first, -1, 0)
            landed(t, 0, slot(t, j), first, 1)
            push(t, 2, slot(t, j, 0), slot(t, j, 0), first, 1)
            push(t, 5, slot(t, j), slot(t, j), second, 1)
            push(t, 9, slot(t, j), slot(t, j), second, -1)

        def e2():
            j = dp_of(first, 1, 0)
            landed(t, 1, slot(t, j), first, -1)
            push(t, 3, slot(t, j, 1), slot(t, j, 1), first, -1)
            push(t, 6, slot(t, j), slot(t, j), second, 1)
            push(t, 10, slot(t, j), slot(t, j), second, -1)

        def e3():
            j = dp_of(first, 2, 0)
            landed(t, 2, slot(t, j, 0), first, 1)
            landed(t, 3, slot(t, j, 1), first, -1)
            push(t, 7, slot(t, j), slot(t, j), second, 1)
            push(t, 11, slot(t, j), slot(t, j), second, -1)

        def forward(k):
            def event():
                j = dp_of(first, offsets[k], -1)
                landed(t, 4 + k, slot(t, j), second, 1)
                push(t, 12 + k, slot(t, j, 0), slot(t, j, 0), second, 1)
                j = dp_of(first, offsets[k], 1)
                landed(t, 8 + k, slot(t, j), second, -1)
                push(t, 16 + k, slot(t, j, 1), slot(t, j, 1), second, -1)
            return event

        def finish(k):
            def event():
                j = dp_of(first, offsets[k], 2)
                landed(t, 12 + k, slot(t, j, 0), second, 1)
                landed(t, 16 + k, slot(t, j, 1), second, -1)
            return event

        return [e0, e0b, e1, e2, forward(0), e3, forward(1), forward(2), finish(0), forward(3),
                finish(1), finish(2), finish(3)]

    events = []
    per = [tree_events(t) for t in range(TREES)]
    for pair in range(TREES // 2):
        a, b = per[2 * pair], per[2 * pair + 1]
        for first_event, second_event in zip(a, b):
            events.append((pair * 1.0, first_event))
            events.append((pair * 1.0, second_event))
    per_pair = len(events) // (TREES // 2)
    SHIFT = 4
    keyed = []
    for i, (p, event) in enumerate(events):
        keyed.append(((i % per_pair) // 2 + SHIFT * p, p, i, event))
    keyed.sort(key=lambda item: item[:3])
    queue = [item[3] for item in keyed]
    total = len(queue)
    done = [0]

    def advance(upto):
        while done[0] < min(upto, total):
            queue[done[0]]()
            done[0] += 1

    mine = pl.ds(core * 64, 64)
    theirs = pl.ds((1 - core) * 64, 64)
    local = pltpu.make_async_copy(picked.at[:, mine], own.at[pl.ds(0, CAP)], keep_sem.at[4])
    local.start()
    mine_out = pltpu.make_async_copy(picked, pool.at[pl.ds(0, CAP)], keep_sem.at[5])
    mine_out.start()
    keeps.append(mine_out)
    swap = remote(picked.at[:, theirs], own.at[pl.ds(CAP, CAP)], pair_send.at[0], pair_recv.at[0], sibling)
    go(swap)
    advance(8)
    local.wait()
    swap.wait_recv()
    whole = remote(picked, pool.at[pl.ds(CAP, CAP)], pair_send.at[1], pair_recv.at[1], sibling)
    lag = table[0]
    saves = []
    for step in range(STEPS + 1):
        if step > 0:
            for way in (0, 1):
                ref = got.at[way, step - 1]
                remote(ref, ref, ring_send.at[way, step - 1], ring_recv.at[way, step - 1],
                       {"enc": enc_at(1 - 2 * way)}).wait_recv()
        if step < STEPS:
            take_own = step < table[1]
            index = table[2 + step]
            for way in (0, 1):
                rows = pl.ds(way * 32, 32)
                value = own[index, rows]
                for back in range(1, 7):
                    if step - back >= 0:
                        use = jnp.logical_and(jnp.logical_not(take_own), lag == back)
                        value = jnp.where(use, got[way, step - back], value)
                staged[way, step] = value
                go(remote(staged.at[way, step], got.at[way, step], ring_send.at[way, step],
                          ring_recv.at[way, step], {"enc": enc_at(1 - 2 * way)}))
        if step > 0:
            for way in (0, 1):
                dst = pool.at[2 * CAP + step - 1, pl.ds(core * 64 + way * 32, 32)]
                save = pltpu.make_async_copy(got.at[way, step - 1], dst, save_sem.at[way, step - 1])
                save.start()
                saves.append(save)
                go(remote(got.at[way, step - 1], dst, pair_send.at[2 + 2 * (step - 1) + way],
                          pair_recv.at[2 + 2 * (step - 1) + way], sibling))
        if step == 1:
            go(whole)
        advance(8 + (total - 8) * (step + 1) // (STEPS + 1))
    advance(total)
    whole.wait_recv()
    for step in range(STEPS):
        for way in (0, 1):
            dst = pool.at[2 * CAP + step, pl.ds((1 - core) * 64 + way * 32, 32)]
            remote(dst, dst, pair_send.at[2 + 2 * step + way], pair_recv.at[2 + 2 * step + way], sibling).wait_recv()
    for copy in keeps + saves:
        copy.wait()
    for copy in sends:
        copy.wait_send()


def gather_all(table, wq, wk, wv, wo, picked):
    return pl.pallas_call(
        gather_kernel,
        out_shape=(jax.ShapeDtypeStruct((4, 16, 256, 256), jnp.bfloat16),
                   jax.ShapeDtypeStruct((2 * CAP + STEPS, 128, 4096), jnp.bfloat16)),
        in_specs=[SMEM] + [ANY] * 5,
        out_specs=(ANY, ANY),
        scratch_shapes=[
            pltpu.VMEM((2 * CAP, 64, 4096), jnp.bfloat16),
            pltpu.VMEM((2, STEPS, 32, 4096), jnp.bfloat16),
            pltpu.VMEM((2, STEPS, 32, 4096), jnp.bfloat16),
            pltpu.SemaphoreType.DMA((TREES * SEMS,)),
            pltpu.SemaphoreType.DMA((TREES * SEMS,)),
            pltpu.SemaphoreType.DMA((6,)),
            pltpu.SemaphoreType.DMA((2, STEPS)),
            pltpu.SemaphoreType.DMA((2, STEPS)),
            pltpu.SemaphoreType.DMA((2, STEPS)),
            pltpu.SemaphoreType.DMA((2 + 2 * STEPS,)),
            pltpu.SemaphoreType.DMA((2 + 2 * STEPS,)),
        ],
        compiler_params=pltpu.CompilerParams(
            collective_id=0, has_side_effects=True, vmem_limit_bytes=48 * 1024 * 1024),
        name="gather_all",
    )(table, wq, wk, wv, wo, picked)


def routes(owners, enc):
    y, core = enc // 2, enc % 2
    count = owners.shape[0]
    places = jnp.arange(count, dtype=jnp.int32)
    chip = owners // 2
    earlier = places[None, :] < places[:, None]
    rank = jnp.sum(((owners[None, :] == owners[:, None]) & earlier).astype(jnp.int32), axis=1)
    chip_rank = jnp.sum(((chip[None, :] == chip[:, None]) & earlier).astype(jnp.int32), axis=1)
    held = jnp.sum((chip[None, :] == jnp.arange(4, dtype=jnp.int32)[:, None]).astype(jnp.int32), axis=1)
    lags = jnp.maximum(held, 1)
    here = chip == y
    n_here = jnp.sum(here.astype(jnp.int32))
    own_index = jnp.where(owners % 2 == core, rank, CAP + rank)
    steps = jnp.arange(STEPS, dtype=jnp.int32)
    match = here[None, :] & (chip_rank[None, :] == steps[:, None])
    order = jnp.sum(jnp.where(match, own_index[None, :], 0), axis=1)
    lag_here = jnp.maximum(n_here, 1)
    table = jnp.concatenate([lag_here[None], n_here[None], order]).astype(jnp.int32)
    spots = []
    for sign in (1, -1):
        hops = (y - chip) * sign % 4
        near = jnp.sum(jnp.where(jnp.arange(4)[None, :] == ((y - sign) % 4), lags[None, :], 0), axis=1)
        mid = jnp.sum(jnp.where(jnp.arange(4)[None, :] == ((y - 2 * sign) % 4), lags[None, :], 0), axis=1)
        spots.append(CAP + chip_rank + jnp.where(hops > 1, near, 0) + jnp.where(hops > 2, mid, 0))
    right = jnp.where(here, own_index, CAP + spots[0])
    left = jnp.where(here, own_index, CAP + spots[1])
    return table, right.astype(jnp.int32), left.astype(jnp.int32)


def pick_kernel(index, store, out):
    out[...] = store[...]


def pick(index, store):
    return pl.pallas_call(
        pick_kernel,
        out_shape=jax.ShapeDtypeStruct((CAP, 128, 4096), jnp.bfloat16),
        grid_spec=pltpu.PrefetchScalarGridSpec(
            num_scalar_prefetch=1,
            grid=(CAP, 2),
            in_specs=[pl.BlockSpec((1, 64, 4096), lambda i, j, index: (index[i], j, 0))],
            out_specs=pl.BlockSpec((1, 64, 4096), lambda i, j, index: (i, j, 0)),
        ),
        name="pick",
    )(index, store)


def my_picks(owners, rows, enc):
    mine = (owners == enc).astype(jnp.int32)
    order = jnp.cumsum(mine) - 1
    slot_ids = jnp.arange(CAP, dtype=jnp.int32)
    chosen = mine[None, :] * (order[None, :] == slot_ids[:, None]).astype(jnp.int32)
    return jnp.sum(chosen * rows[None, :], axis=1).astype(jnp.int32)


def add_to(dst, *parts):
    value = dst[...].astype(jnp.float32)
    for part in parts:
        value += part[...].astype(jnp.float32)
    dst[...] = value.astype(jnp.bfloat16)


def reduce_kernel(small, dkt, dvt, rows_in, tok_in, cot_in, weights,
                  cca, gtok, gq, gk, gv, go_out,
                  x, tok, cot, wq, wo, lhs, terms, outs, half1, full1, half2, full2,
                  pair_got, ring_half, ring_full,
                  load_sem, tree_send, tree_recv, out_send, out_recv):
    px, pz, py, core = place()

    def dp_at(axis, by):
        if axis == 0:
            return around(px, by) * 4 + pz
        return px * 4 + around(pz, by)

    def dp_of(first, o1, o2):
        if first == 0:
            return around(px, o1) * 4 + around(pz, o2)
        return around(px, o2) * 4 + around(pz, o1)

    def enc_at(by):
        return around(py, by) * 2 + core

    sibling = {"enc": py * 2 + 1 - core}
    loads = {}
    for i, (name, src, dst) in enumerate((
            ("small", small, lhs), ("cot", cot_in, cot), ("wo", weights.at[3], wo),
            ("x", rows_in, x), ("tok", tok_in, tok), ("wq", weights.at[0], wq))):
        loads[name] = pltpu.make_async_copy(src, dst, load_sem.at[i])
        loads[name].start()
    greet([{"dp": dp_at(a, b)} for a in (0, 1) for b in (1, -1)]
          + [{"enc": enc_at(1)}, {"enc": enc_at(-1)}, sibling])

    sends = []

    def go(copy):
        copy.start()
        sends.append(copy)

    def fill(w, left, right, chunk=256):
        def step(j, carry):
            cols = pl.ds(pl.multiple_of(j * 256, 256), 256)
            terms[w, j] = jnp.dot(left[...], right[:, cols], preferred_element_type=jnp.float32).astype(jnp.bfloat16)
            return carry
        lax.fori_loop(0, 16, step, 0)

    def fill_out(u, left, weight, flip):
        dims = (((1,), (1 if flip else 0,)), ((), ()))

        def step(j, carry):
            e = j // 2
            value = lax.dot_general(left[...], weight[j], dims, preferred_element_type=jnp.float32)
            cols = pl.ds(pl.multiple_of((j % 2) * 256, 256), 256)
            outs[u, e % 2, e // 2, :, cols] = value.astype(jnp.bfloat16)
            return carry
        lax.fori_loop(0, 16, step, 0)

    offsets = (2, -1, 1, 0)

    def tree(w, h):
        t = 2 * w + h
        first, second = h, 1 - h
        r0 = h * 128

        def block(o1, o2, part=None):
            j = dp_of(first, o1, o2)
            if part is None:
                return terms.at[w, j, pl.ds(r0, 128)]
            return terms.at[w, j, pl.ds(r0 + 64 * part, 64)]

        def push(k, src, dst, axis, by):
            go(remote(src, dst, tree_send.at[t * SEMS + k], tree_recv.at[t * SEMS + k], {"dp": dp_at(axis, by)}))

        def landed(k, dst, axis, by):
            remote(dst, dst, tree_send.at[t * SEMS + k], tree_recv.at[t * SEMS + k],
                   {"dp": dp_at(axis, by)}).wait_recv()

        def s1(k):
            def event():
                push(4 * k, block(offsets[k], 2, 0), half1.at[t, k, 0], second, 1)
                push(4 * k + 1, block(offsets[k], 2, 1), half1.at[t, k, 1], second, -1)
            return event

        def s2(k):
            def event():
                landed(4 * k, half1.at[t, k, 0], second, 1)
                add_to(block(offsets[k], 1, 0), half1.at[t, k, 0])
                push(4 * k + 2, block(offsets[k], 1), full1.at[t, k, 0], second, 1)
                landed(4 * k + 1, half1.at[t, k, 1], second, -1)
                add_to(block(offsets[k], -1, 1), half1.at[t, k, 1])
                push(4 * k + 3, block(offsets[k], -1), full1.at[t, k, 1], second, -1)
            return event

        def s3(k):
            def event():
                landed(4 * k + 2, full1.at[t, k, 0], second, 1)
                landed(4 * k + 3, full1.at[t, k, 1], second, -1)
                add_to(block(offsets[k], 0), full1.at[t, k, 0], full1.at[t, k, 1])
            return event

        def s4():
            push(16, block(2, 0, 0), half2.at[t, 0], first, 1)
            push(17, block(2, 0, 1), half2.at[t, 1], first, -1)

        def s5():
            landed(16, half2.at[t, 0], first, 1)
            add_to(block(1, 0, 0), half2.at[t, 0])
            push(18, block(1, 0), full2.at[t, 0], first, 1)
            landed(17, half2.at[t, 1], first, -1)
            add_to(block(-1, 0, 1), half2.at[t, 1])
            push(19, block(-1, 0), full2.at[t, 1], first, -1)

        def s6():
            landed(18, full2.at[t, 0], first, 1)
            landed(19, full2.at[t, 1], first, -1)
            value = (block(0, 0)[...].astype(jnp.float32) + full2[t, 0].astype(jnp.float32)
                     + full2[t, 1].astype(jnp.float32))
            if w == 3:
                go_out[pl.ds(r0, 128), :] = value.astype(jnp.bfloat16)
            else:
                (gq, gk, gv)[w][:, pl.ds(r0, 128)] = value.T.astype(jnp.bfloat16)

        return [s1(0), s1(1), s1(2), s1(3)], [
            s2(0), s2(1), s2(2), s2(3), s3(0), s4, s3(1), s3(2), s5, s3(3), s6]

    def output(u, final):
        def push(k, src, dst, target):
            go(remote(src, dst, out_send.at[u * 5 + k], out_recv.at[u * 5 + k], target))

        def landed(k, dst, target):
            remote(dst, dst, out_send.at[u * 5 + k], out_recv.at[u * 5 + k], target).wait_recv()

        ahead, behind = {"enc": enc_at(1)}, {"enc": enc_at(-1)}
        top, bottom = pl.ds(0, 128), pl.ds(128, 128)

        def block(by, part=None):
            if part is None:
                return outs.at[u, core, around(py, by)]
            return outs.at[u, core, around(py, by), (top, bottom)[part]]

        def p0():
            push(0, outs.at[u, 1 - core], pair_got.at[u], sibling)

        def p1():
            landed(0, pair_got.at[u], sibling)
            add_to(block(2), pair_got.at[u, around(py, 2)])
            push(1, block(2, 0), ring_half.at[u, 0], ahead)
            push(2, block(2, 1), ring_half.at[u, 1], behind)
            for by in (1, -1, 0):
                add_to(block(by), pair_got.at[u, around(py, by)])

        def p2():
            landed(1, ring_half.at[u, 0], ahead)
            add_to(block(1, 0), ring_half.at[u, 0])
            push(3, block(1), ring_full.at[u, 0], ahead)
            landed(2, ring_half.at[u, 1], behind)
            add_to(block(-1, 1), ring_half.at[u, 1])
            push(4, block(-1), ring_full.at[u, 1], behind)

        def p3():
            landed(3, ring_full.at[u, 0], ahead)
            landed(4, ring_full.at[u, 1], behind)
            value = (block(0)[...].astype(jnp.float32) + ring_full[u, 0].astype(jnp.float32)
                     + ring_full[u, 1].astype(jnp.float32))
            final[...] = value.astype(jnp.bfloat16)

        return [p0, p1, p2, p3]

    outs0, outs1 = output(0, cca), output(1, gtok)
    lists = {w: (tree(w, 0), tree(w, 1)) for w in (3, 2, 1, 0)}

    def begin(w):
        for k in range(4):
            lists[w][0][0][k]()
            lists[w][1][0][k]()

    def then(w, lo, hi):
        for k in range(lo, hi):
            lists[w][0][1][k]()
            lists[w][1][1][k]()

    loads["small"].wait()
    loads["cot"].wait()
    fill(3, lhs.at[2], cot)
    begin(3)
    loads["wo"].wait()
    fill_out(0, lhs.at[0], wo, False)
    outs0[0]()
    loads["x"].wait()
    fill(2, dvt, x)
    begin(2)
    then(3, 0, 4)
    fill(1, dkt, x)
    begin(1)
    outs0[1]()
    loads["tok"].wait()
    fill(0, lhs.at[3], tok)
    begin(0)
    loads["wq"].wait()
    fill_out(1, lhs.at[1], wq, True)
    outs1[0]()
    then(2, 0, 4)
    outs0[2]()
    outs1[1]()
    then(3, 4, 8)
    then(1, 0, 4)
    then(0, 0, 4)
    outs1[2]()
    outs0[3]()
    then(3, 8, 10)
    then(2, 4, 8)
    then(1, 4, 8)
    then(2, 8, 10)
    then(0, 4, 8)
    outs1[3]()
    then(1, 8, 10)
    then(3, 10, 11)
    then(0, 8, 10)
    then(2, 10, 11)
    then(1, 10, 11)
    then(0, 10, 11)
    for copy in sends:
        copy.wait_send()


def reduce_all(small, dkt, dvt, rows_in, tokens, cotangent, weights):
    bf = jnp.bfloat16
    return pl.pallas_call(
        reduce_kernel,
        out_shape=(jax.ShapeDtypeStruct((256, 512), bf), jax.ShapeDtypeStruct((256, 512), bf),
                   jax.ShapeDtypeStruct((256, 256), bf), jax.ShapeDtypeStruct((256, 256), bf),
                   jax.ShapeDtypeStruct((256, 256), bf), jax.ShapeDtypeStruct((256, 256), bf)),
        in_specs=[ANY, VMEM, VMEM, ANY, ANY, ANY, ANY],
        out_specs=(VMEM,) * 6,
        scratch_shapes=[
            pltpu.VMEM((1024, 4096), bf),
            pltpu.VMEM((256, 4096), bf),
            pltpu.VMEM((256, 4096), bf),
            pltpu.VMEM((16, 256, 256), bf),
            pltpu.VMEM((16, 256, 256), bf),
            pltpu.VMEM((4, 256, 256), bf),
            pltpu.VMEM((4, 16, 256, 256), bf),
            pltpu.VMEM((2, 2, 4, 256, 512), bf),
            pltpu.VMEM((TREES, 4, 2, 64, 256), bf),
            pltpu.VMEM((TREES, 4, 2, 128, 256), bf),
            pltpu.VMEM((TREES, 2, 64, 256), bf),
            pltpu.VMEM((TREES, 2, 128, 256), bf),
            pltpu.VMEM((2, 4, 256, 512), bf),
            pltpu.VMEM((2, 2, 128, 512), bf),
            pltpu.VMEM((2, 2, 256, 512), bf),
            pltpu.SemaphoreType.DMA((6,)),
            pltpu.SemaphoreType.DMA((TREES * SEMS,)),
            pltpu.SemaphoreType.DMA((TREES * SEMS,)),
            pltpu.SemaphoreType.DMA((10,)),
            pltpu.SemaphoreType.DMA((10,)),
        ],
        compiler_params=pltpu.CompilerParams(
            collective_id=1, has_side_effects=True, vmem_limit_bytes=56 * 1024 * 1024),
        name="reduce_all",
    )(small, dkt, dvt, rows_in, tokens, cotangent, weights)


def attend_kernel(right, left, pool, weights, tok_in, cot_in,
                  rows_out, small, dkt, dvt,
                  x, tok, cot, w, q, k, v, dm, load_sem, save_sem):
    scale = 1.0 / math.sqrt(HD)
    f32, bf = jnp.float32, jnp.bfloat16
    tok_load = pltpu.make_async_copy(tok_in, tok, load_sem.at[0])
    cot_load = pltpu.make_async_copy(cot_in, cot, load_sem.at[1])
    w_loads = [pltpu.make_async_copy(weights.at[i], w.at[i], load_sem.at[2 + i]) for i in range(4)]

    def part(n, p):
        index = (right, left)[p % 2][n]
        return pltpu.make_async_copy(pool.at[index, pl.ds(32 * p, 32)], x.at[n, pl.ds(32 * p, 32)],
                                     load_sem.at[6 + 4 * n + p])

    parts = [[part(n, p) for p in range(4)] for n in range(8)]
    w_loads[1].start()
    for n in range(2):
        for copy in parts[n]:
            copy.start()
    w_loads[2].start()
    for n in range(2, 8):
        for copy in parts[n]:
            copy.start()
    tok_load.start()
    w_loads[0].start()
    cot_load.start()
    w_loads[3].start()
    saves = []
    w_loads[1].wait()
    for c in range(4):
        for n in (2 * c, 2 * c + 1):
            for copy in parts[n]:
                copy.wait()
            save = pltpu.make_async_copy(x.at[n], rows_out.at[n], save_sem.at[n])
            save.start()
            saves.append(save)
        if c == 0:
            w_loads[2].wait()
        keyrows = x[2 * c:2 * c + 2].reshape(256, 4096)
        k[c] = jnp.dot(keyrows, w[1].reshape(4096, 256), preferred_element_type=f32).astype(bf)
        v[c] = jnp.dot(keyrows, w[2].reshape(4096, 256), preferred_element_type=f32).astype(bf)
    tok_load.wait()
    w_loads[0].wait()
    q[...] = jnp.dot(tok[...], w[0].reshape(4096, 256), preferred_element_type=f32).astype(bf)
    cot_load.wait()
    w_loads[3].wait()
    acc = jnp.zeros((256, 256), f32)
    nt = (((1,), (1,)), ((), ()))
    tn = (((0,), (0,)), ((), ()))
    for j in range(16):
        acc += lax.dot_general(cot[:, 256 * j:256 * j + 256], w[3, j], nt, preferred_element_type=f32)
    dm[...] = acc.astype(bf)
    for c in range(4):
        t = slice(64 * c, 64 * c + 64)
        for h in range(2):
            e = slice(128 * h, 128 * h + 128)
            qc, kc, vc, dc = q[t, e], k[c, :, e], v[c, :, e], dm[t, e]
            s = lax.dot_general(qc, kc, nt, preferred_element_type=f32) * scale
            p = jnp.exp(s - jnp.max(s, axis=-1, keepdims=True))
            p = p / jnp.sum(p, axis=-1, keepdims=True)
            pb = p.astype(bf)
            dp = lax.dot_general(dc, vc, nt, preferred_element_type=f32)
            ds = (p * (dp - jnp.sum(dp * p, axis=-1, keepdims=True)) * scale).astype(bf)
            small[0, t, e] = jnp.dot(pb, vc, preferred_element_type=f32).astype(bf)
            small[1, t, e] = jnp.dot(ds, kc, preferred_element_type=f32).astype(bf)
            dkt[e, 256 * c:256 * c + 256] = lax.dot_general(qc, ds, tn, preferred_element_type=f32).astype(bf)
            dvt[e, 256 * c:256 * c + 256] = lax.dot_general(dc, pb, tn, preferred_element_type=f32).astype(bf)
    small[2] = small[0].astype(f32).T.astype(bf)
    small[3] = small[1].astype(f32).T.astype(bf)
    for save in saves:
        save.wait()


def attend(right, left, pool, weights, tokens, cotangent):
    bf = jnp.bfloat16
    return pl.pallas_call(
        attend_kernel,
        out_shape=(jax.ShapeDtypeStruct((8, 128, 4096), bf), jax.ShapeDtypeStruct((4, 256, 256), bf),
                   jax.ShapeDtypeStruct((256, 1024), bf), jax.ShapeDtypeStruct((256, 1024), bf)),
        in_specs=[SMEM, SMEM, ANY, ANY, ANY, ANY],
        out_specs=(ANY, VMEM, VMEM, VMEM),
        scratch_shapes=[
            pltpu.VMEM((8, 128, 4096), bf),
            pltpu.VMEM((256, 4096), bf),
            pltpu.VMEM((256, 4096), bf),
            pltpu.VMEM((4, 16, 256, 256), bf),
            pltpu.VMEM((256, 256), bf),
            pltpu.VMEM((4, 256, 256), bf),
            pltpu.VMEM((4, 256, 256), bf),
            pltpu.VMEM((256, 256), bf),
            pltpu.SemaphoreType.DMA((38,)),
            pltpu.SemaphoreType.DMA((8,)),
        ],
        compiler_params=pltpu.CompilerParams(vmem_limit_bytes=48 * 1024 * 1024),
        name="attend",
    )(right, left, pool, weights, tokens, cotangent)


def body(tokens, store, holder, rows, wq, wk, wv, wo, cotangent):
    enc = lax.axis_index("enc")
    owners = holder[:, 0]
    table, right, left = routes(owners, enc)
    picked = pick(my_picks(owners, rows, enc), store)
    weights, pool = gather_all(table, wq, wk, wv, wo, picked)
    keyrows, small, dkt, dvt = attend(right, left, pool, weights, tokens, cotangent)
    return reduce_all(small, dkt, dvt, keyrows.reshape(1024, 4096), tokens, cotangent, weights)


def solution(mesh):
    placed = (
        P("dp", None), P(("dp", "enc"), None, None), P("dp", None), P("dp"),
        P("dp", "enc"), P("dp", "enc"), P("dp", "enc"), P("enc", "dp"), P("dp", None),
    )
    return jax.shard_map(
        body, mesh=mesh, in_specs=placed,
        out_specs=(P("dp", "enc"),) * 5 + (P("enc", "dp"),),
        check_vma=False,
    )
```

```python
import functools
import math

import jax
import jax.numpy as jnp
from jax import lax
from jax.experimental import pallas as pl
from jax.experimental.pallas import tpu as pltpu
from jax.sharding import PartitionSpec as P

ANY = pl.BlockSpec(memory_space=pl.ANY)
VMEM = pl.BlockSpec(memory_space=pltpu.VMEM)
SMEM = pl.BlockSpec(memory_space=pltpu.SMEM)
HD = 128
CAP = 3
STEPS = 9
SUBS = 2
SUB = 32 // SUBS
TREES = 8
SEMS = 20
STAGES = 9
NT = (((1,), (1,)), ((), ()))
TN = (((0,), (0,)), ((), ()))


def place():
    dp = lax.axis_index("dp")
    enc = lax.axis_index("enc")
    return dp // 4, dp % 4, enc // 2, enc % 2


def around(value, by):
    return lax.rem(value + (4 + by), 4)


def remote(src, dst, send, recv, target):
    return pltpu.make_async_remote_copy(
        src_ref=src, dst_ref=dst, send_sem=send, recv_sem=recv,
        device_id=target, device_id_type=pl.DeviceIdType.MESH,
    )


def greet(peers):
    barrier = pltpu.get_barrier_semaphore()
    for peer in peers:
        pl.semaphore_signal(barrier, inc=1, device_id=peer, device_id_type=pl.DeviceIdType.MESH)
    pl.semaphore_wait(barrier, len(peers))


def count_if(flag):
    return jnp.where(flag, 1, 0)


def routes(holder, rows, y, core):
    owner = [holder[n, 0] for n in range(8)]
    row = [rows[n] for n in range(8)]
    chip = [o // 2 for o in owner]
    here = [c == y for c in chip]
    rank, chip_rank = [], []
    for n in range(8):
        a, b = jnp.int32(0), jnp.int32(0)
        for m in range(n):
            a += count_if(owner[m] == owner[n])
            b += count_if(chip[m] == chip[n])
        rank.append(a)
        chip_rank.append(b)
    picks = []
    for k in range(CAP):
        value = jnp.int32(0)
        for n in range(8):
            value += jnp.where(jnp.logical_and(owner[n] == y * 2 + core, rank[n] == k), row[n], 0)
        picks.append(value)
    capped = [jnp.minimum(r, CAP - 1) for r in rank]
    own_index = [jnp.where(owner[n] % 2 == core, capped[n], CAP + capped[n]) for n in range(8)]
    order = []
    for t in range(2 * CAP):
        value = jnp.int32(0)
        for n in range(8):
            value += jnp.where(jnp.logical_and(here[n], chip_rank[n] == t), own_index[n], 0)
        order.append(value)

    def held(c):
        value = jnp.int32(0)
        for n in range(8):
            value += count_if(chip[n] == c)
        return value

    n_here = held(y)
    spots = []
    for sign in (1, -1):
        near = jnp.maximum(held(around(y, -sign)), 1)
        mid = jnp.maximum(held(around(y, -2 * sign)), 1)
        spot = []
        for n in range(8):
            hops = lax.rem((y - chip[n]) * sign + 4, 4)
            at = chip_rank[n] + jnp.where(hops > 1, near, 0) + jnp.where(hops > 2, mid, 0)
            spot.append(jnp.minimum(at, STEPS - 1))
        spots.append(spot)
    return picks, order, n_here, here, own_index, spots


def gather_kernel(holder, rows_in, store, wk, wv, wq, wo, tok_in, cot_in,
                  rows_out, small, dkt, dvt, wq_out, wo_out,
                  near, far, own_near, own_far, got, staged, weights, tok, cot,
                  kown_near, kown_far, kgot, vown_near, vown_far, vgot, q, k, v, dm,
                  load_sem, tree_send, tree_recv, ring_send, ring_recv, pair_send, pair_recv,
                  own_send, own_recv, save_sem):
    f32, bf = jnp.float32, jnp.bfloat16
    x, z, y, core = place()
    dp = x * 4 + z
    sources = (wk, wv, wq, wo)

    def dp_at(axis, by):
        if axis == 0:
            return around(x, by) * 4 + z
        return x * 4 + around(z, by)

    def dp_of(first, o1, o2):
        if first == 0:
            return around(x, o1) * 4 + around(z, o2)
        return around(x, o2) * 4 + around(z, o1)

    def enc_at(by):
        return around(y, by) * 2 + core

    sibling = {"enc": y * 2 + 1 - core}
    mine = pl.ds(core * 64, 64)
    theirs = pl.ds((1 - core) * 64, 64)
    load_far = pltpu.make_async_copy(store.at[:, theirs], far, load_sem.at[0])
    load_near = pltpu.make_async_copy(store.at[:, mine], near, load_sem.at[1])
    load_far.start()
    load_near.start()
    keeps = []
    for i in range(4):
        copy = pltpu.make_async_copy(sources[i], weights.at[i, dp], load_sem.at[2 + i])
        copy.start()
        keeps.append(copy)
    load_tok = pltpu.make_async_copy(tok_in, tok, load_sem.at[6])
    load_cot = pltpu.make_async_copy(cot_in, cot, load_sem.at[7])
    greet([{"dp": dp_at(a, b)} for a in (0, 1) for b in (1, -1)]
          + [{"enc": enc_at(1)}, {"enc": enc_at(-1)}, sibling])

    sends = []

    def go(copy):
        copy.start()
        sends.append(copy)

    half = 128
    quarter = half // 2

    def slot(t, j, part=None):
        r0 = (t % 2) * half
        if part is None:
            return weights.at[t // 2, j, pl.ds(r0, half)]
        return weights.at[t // 2, j, pl.ds(r0 + part * quarter, quarter)]

    def push(t, i, src, dst, axis, by):
        go(remote(src, dst, tree_send.at[t * SEMS + i], tree_recv.at[t * SEMS + i], {"dp": dp_at(axis, by)}))

    def landed(t, i, dst, axis, by):
        remote(dst, dst, tree_send.at[t * SEMS + i], tree_recv.at[t * SEMS + i], {"dp": dp_at(axis, by)}).wait_recv()

    offsets = (0, -1, 1, 2)

    def tree_events(t):
        first = t % 2
        second = 1 - first
        own_half = sources[t // 2].at[pl.ds((t % 2) * half, half)]

        def e0():
            push(t, 0, own_half, slot(t, dp), first, 1)
            push(t, 1, own_half, slot(t, dp), first, -1)

        def e0b():
            push(t, 4, own_half, slot(t, dp), second, 1)
            push(t, 8, own_half, slot(t, dp), second, -1)

        def e1():
            j = dp_of(first, -1, 0)
            landed(t, 0, slot(t, j), first, 1)
            push(t, 2, slot(t, j, 0), slot(t, j, 0), first, 1)
            push(t, 5, slot(t, j), slot(t, j), second, 1)
            push(t, 9, slot(t, j), slot(t, j), second, -1)

        def e2():
            j = dp_of(first, 1, 0)
            landed(t, 1, slot(t, j), first, -1)
            push(t, 3, slot(t, j, 1), slot(t, j, 1), first, -1)
            push(t, 6, slot(t, j), slot(t, j), second, 1)
            push(t, 10, slot(t, j), slot(t, j), second, -1)

        def e3():
            j = dp_of(first, 2, 0)
            landed(t, 2, slot(t, j, 0), first, 1)
            landed(t, 3, slot(t, j, 1), first, -1)
            push(t, 7, slot(t, j), slot(t, j), second, 1)
            push(t, 11, slot(t, j), slot(t, j), second, -1)

        def forward(i):
            def event():
                j = dp_of(first, offsets[i], -1)
                landed(t, 4 + i, slot(t, j), second, 1)
                push(t, 12 + i, slot(t, j, 0), slot(t, j, 0), second, 1)
                j = dp_of(first, offsets[i], 1)
                landed(t, 8 + i, slot(t, j), second, -1)
                push(t, 16 + i, slot(t, j, 1), slot(t, j, 1), second, -1)
            return event

        def finish(i):
            def event():
                j = dp_of(first, offsets[i], 2)
                landed(t, 12 + i, slot(t, j, 0), second, 1)
                landed(t, 16 + i, slot(t, j, 1), second, -1)
            return event

        return [e0, e0b, e1, e2, forward(0), e3, forward(1), forward(2), finish(0), forward(3),
                finish(1), finish(2), finish(3)]

    per = [tree_events(t) for t in range(TREES)]
    keyed = []
    for w in range(4):
        for i in range(13):
            for h in range(2):
                keyed.append((i + 4 * w, w, i, h))
    keyed.sort()
    queue = [per[2 * w + h][i] for _, w, i, h in keyed]
    ends = {w: keyed.index((12 + 4 * w, w, 12, 1)) + 1 for w in range(4)}
    total = len(queue)
    done = [0]

    def advance(upto):
        while done[0] < min(upto, total):
            queue[done[0]]()
            done[0] += 1

    advance(4)
    picks, order, n_here, here, own_index, spots = routes(holder, rows_in, y, core)
    lag = jnp.maximum(n_here, 1)
    load_far.wait()
    for i in range(CAP):
        own_far[i] = far[picks[i]]
    swap = remote(own_far.at[pl.ds(0, CAP)], own_near.at[pl.ds(CAP, CAP)], own_send.at[0], own_recv.at[0], sibling)
    go(swap)
    load_near.wait()
    for i in range(CAP):
        own_near[i] = near[picks[i]]
    load_tok.start()
    load_cot.start()
    advance(8)
    swap.wait_recv()
    swap_back = remote(own_near.at[pl.ds(0, CAP)], own_far.at[pl.ds(CAP, CAP)], own_send.at[1], own_recv.at[1], sibling)

    def lane(of, way, sub):
        return pl.ds(of * 64 + way * 32 + sub * SUB, SUB)

    def pair_wait(step):
        for way in (0, 1):
            for sub in range(SUBS):
                ref = got.at[step, lane(1 - core, way, sub)]
                remote(ref, ref, pair_send.at[step, way, sub], pair_recv.at[step, way, sub], sibling).wait_recv()

    def project(w, value):
        return jnp.dot(value, weights[w].reshape(4096, 256), preferred_element_type=f32).astype(bf)

    def kv_own():
        advance(ends[1])
        for copy in keeps[:2]:
            copy.wait()
        kown_near[...] = project(0, own_near[...].reshape(384, 4096)).reshape(6, 64, 256)
        vown_near[...] = project(1, own_near[...].reshape(384, 4096)).reshape(6, 64, 256)

    def kv_far():
        swap_back.wait_recv()
        kown_far[...] = project(0, own_far[...].reshape(384, 4096)).reshape(6, 64, 256)
        vown_far[...] = project(1, own_far[...].reshape(384, 4096)).reshape(6, 64, 256)

    def kv_got(lo, hi):
        def event():
            for step in range(lo, hi):
                pair_wait(step)
            m = (hi - lo) * 128
            value = got[lo:hi].reshape(m, 4096)
            kgot[lo:hi] = project(0, value).reshape(hi - lo, 128, 256)
            vgot[lo:hi] = project(1, value).reshape(hi - lo, 128, 256)
        return event

    def queries():
        advance(ends[2])
        keeps[2].wait()
        load_tok.wait()
        q[...] = project(2, tok[...])

    def upstream():
        advance(ends[3])
        keeps[3].wait()
        load_cot.wait()
        acc = jnp.zeros((256, 256), f32)
        for j in range(16):
            acc += lax.dot_general(cot[:, 256 * j:256 * j + 256], weights[3, j], NT, preferred_element_type=f32)
        dm[...] = acc.astype(bf)

    work = {10: kv_own, 11: kv_far, 12: kv_got(0, 2), 13: kv_got(2, 4), 15: queries, 16: kv_got(4, 6),
            18: upstream, 19: kv_got(6, 8)}
    for step in range(STEPS + 1):
        for sub in range(SUBS):
            for way in (0, 1):
                toward = {"enc": enc_at(1 - 2 * way)}
                if step > 0:
                    ref = got.at[step - 1, lane(core, way, sub)]
                    remote(ref, ref, ring_send.at[step - 1, way, sub], ring_recv.at[step - 1, way, sub], toward).wait_recv()
                if step < STEPS:
                    rows = pl.ds(way * 32 + sub * SUB, SUB)
                    value = own_near[order[min(step, 5)], rows]
                    for back in range(1, 7):
                        if step - back >= 0:
                            use = jnp.logical_and(n_here <= step, lag == back)
                            value = jnp.where(use, got[step - back, lane(core, way, sub)], value)
                    staged[step, way, sub] = value
                    go(remote(staged.at[step, way, sub], got.at[step, lane(core, way, sub)],
                              ring_send.at[step, way, sub], ring_recv.at[step, way, sub], toward))
                if step > 0:
                    ref = got.at[step - 1, lane(core, way, sub)]
                    go(remote(ref, ref, pair_send.at[step - 1, way, sub], pair_recv.at[step - 1, way, sub], sibling))
            if step == 1 and sub == 0:
                go(swap_back)
            s = SUBS * step + sub
            advance(8 + (total - 8) * (s + 1) // 17)
            if s in work:
                work[s]()
    advance(total)
    saves = [pltpu.make_async_copy(weights.at[2], wq_out, save_sem.at[0]),
             pltpu.make_async_copy(weights.at[3], wo_out, save_sem.at[1])]
    for copy in saves:
        copy.start()
    kv_got(8, 9)()

    for n in range(8):
        for way in (0, 1):
            part = pl.ds(way * 32, 32)
            at = spots[way][n]
            for dst, a, kb, vb, of in ((near, own_near, kown_near, vown_near, core),
                                       (far, own_far, kown_far, vown_far, 1 - core)):
                full = pl.ds(of * 64 + way * 32, 32)
                dst[n, part] = jnp.where(here[n], a[own_index[n], part], got[at, full])
                full_out = pl.ds((n % 2) * 128 + of * 64 + way * 32, 32)
                k[n // 2, full_out] = jnp.where(here[n], kb[own_index[n], part], kgot[at, full])
                v[n // 2, full_out] = jnp.where(here[n], vb[own_index[n], part], vgot[at, full])
    saves += [pltpu.make_async_copy(near, rows_out.at[:, mine], save_sem.at[2]),
              pltpu.make_async_copy(far, rows_out.at[:, theirs], save_sem.at[3])]
    saves[2].start()
    saves[3].start()

    scale = 1.0 / math.sqrt(HD)
    for c in range(4):
        t = slice(64 * c, 64 * c + 64)
        for h in range(2):
            e = slice(128 * h, 128 * h + 128)
            qc, kc, vc, dc = q[t, e], k[c, :, e], v[c, :, e], dm[t, e]
            s = lax.dot_general(qc, kc, NT, preferred_element_type=f32) * scale
            p = jnp.exp(s - jnp.max(s, axis=-1, keepdims=True))
            p = p / jnp.sum(p, axis=-1, keepdims=True)
            pb = p.astype(bf)
            dprob = lax.dot_general(dc, vc, NT, preferred_element_type=f32)
            ds = (p * (dprob - jnp.sum(dprob * p, axis=-1, keepdims=True)) * scale).astype(bf)
            small[0, t, e] = jnp.dot(pb, vc, preferred_element_type=f32).astype(bf)
            small[1, t, e] = jnp.dot(ds, kc, preferred_element_type=f32).astype(bf)
            dkt[e, 256 * c:256 * c + 256] = lax.dot_general(qc, ds, TN, preferred_element_type=f32).astype(bf)
            dvt[e, 256 * c:256 * c + 256] = lax.dot_general(dc, pb, TN, preferred_element_type=f32).astype(bf)
    small[2] = small[0].astype(f32).T.astype(bf)
    small[3] = small[1].astype(f32).T.astype(bf)
    for copy in saves:
        copy.wait()
    for copy in sends:
        copy.wait_send()


def gather_all(holder, rows, store, wk, wv, wq, wo, tokens, cotangent):
    bf = jnp.bfloat16
    dma = pltpu.SemaphoreType.DMA
    return pl.pallas_call(
        gather_kernel,
        out_shape=(jax.ShapeDtypeStruct((8, 128, 4096), bf), jax.ShapeDtypeStruct((4, 256, 256), bf),
                   jax.ShapeDtypeStruct((256, 1024), bf), jax.ShapeDtypeStruct((256, 1024), bf),
                   jax.ShapeDtypeStruct((16, 256, 256), bf), jax.ShapeDtypeStruct((16, 256, 256), bf)),
        in_specs=[SMEM, SMEM] + [ANY] * 7,
        out_specs=(ANY, VMEM, VMEM, VMEM, ANY, ANY),
        scratch_shapes=[
            pltpu.VMEM((8, 64, 4096), bf),
            pltpu.VMEM((8, 64, 4096), bf),
            pltpu.VMEM((2 * CAP, 64, 4096), bf),
            pltpu.VMEM((2 * CAP, 64, 4096), bf),
            pltpu.VMEM((STEPS, 128, 4096), bf),
            pltpu.VMEM((STAGES, 2, SUBS, SUB, 4096), bf),
            pltpu.VMEM((4, 16, 256, 256), bf),
            pltpu.VMEM((256, 4096), bf),
            pltpu.VMEM((256, 4096), bf),
            pltpu.VMEM((2 * CAP, 64, 256), bf),
            pltpu.VMEM((2 * CAP, 64, 256), bf),
            pltpu.VMEM((STEPS, 128, 256), bf),
            pltpu.VMEM((2 * CAP, 64, 256), bf),
            pltpu.VMEM((2 * CAP, 64, 256), bf),
            pltpu.VMEM((STEPS, 128, 256), bf),
            pltpu.VMEM((256, 256), bf),
            pltpu.VMEM((4, 256, 256), bf),
            pltpu.VMEM((4, 256, 256), bf),
            pltpu.VMEM((256, 256), bf),
            dma((8,)),
            dma((TREES * SEMS,)),
            dma((TREES * SEMS,)),
            dma((STEPS, 2, SUBS)),
            dma((STEPS, 2, SUBS)),
            dma((STEPS, 2, SUBS)),
            dma((STEPS, 2, SUBS)),
            dma((2,)),
            dma((2,)),
            dma((4,)),
        ],
        compiler_params=pltpu.CompilerParams(
            collective_id=0, has_side_effects=True, vmem_limit_bytes=60 * 1024 * 1024),
        name="gather_all",
    )(holder, rows, store, wk, wv, wq, wo, tokens, cotangent)


def add_to(dst, *parts):
    value = dst[...].astype(jnp.float32)
    for part in parts:
        value += part[...].astype(jnp.float32)
    dst[...] = value.astype(jnp.bfloat16)


def reduce_kernel(small, dkt_in, dvt_in, rows_in, tok_in, cot_in, wq_in, wo_in,
                  wide, square,
                  x, tok, cot, wq, wo, lhs, dkt, dvt, terms, outs, half1, full1, half2, full2,
                  pair_got, ring_half, ring_full,
                  load_sem, tree_send, tree_recv, out_send, out_recv):
    px, pz, py, core = place()

    def dp_at(axis, by):
        if axis == 0:
            return around(px, by) * 4 + pz
        return px * 4 + around(pz, by)

    def dp_of(first, o1, o2):
        if first == 0:
            return around(px, o1) * 4 + around(pz, o2)
        return around(px, o2) * 4 + around(pz, o1)

    def enc_at(by):
        return around(py, by) * 2 + core

    sibling = {"enc": py * 2 + 1 - core}
    loads = {}
    for i, (name, src, dst) in enumerate((
            ("small", small, lhs), ("cot", cot_in, cot), ("wo", wo_in, wo), ("dvt", dvt_in, dvt),
            ("x", rows_in, x), ("dkt", dkt_in, dkt), ("tok", tok_in, tok), ("wq", wq_in, wq))):
        loads[name] = pltpu.make_async_copy(src, dst, load_sem.at[i])
        loads[name].start()
    greet([{"dp": dp_at(a, b)} for a in (0, 1) for b in (1, -1)]
          + [{"enc": enc_at(1)}, {"enc": enc_at(-1)}, sibling])

    sends = []

    def go(copy):
        copy.start()
        sends.append(copy)

    def fill(w, left, right, chunk=256):
        def step(j, carry):
            cols = pl.ds(pl.multiple_of(j * 256, 256), 256)
            terms[w, j] = jnp.dot(left[...], right[:, cols], preferred_element_type=jnp.float32).astype(jnp.bfloat16)
            return carry
        lax.fori_loop(0, 16, step, 0)

    def fill_out(u, left, weight, flip):
        dims = (((1,), (1 if flip else 0,)), ((), ()))

        def step(j, carry):
            e = j // 2
            value = lax.dot_general(left[...], weight[j], dims, preferred_element_type=jnp.float32)
            cols = pl.ds(pl.multiple_of((j % 2) * 256, 256), 256)
            outs[u, e % 2, e // 2, :, cols] = value.astype(jnp.bfloat16)
            return carry
        lax.fori_loop(0, 16, step, 0)

    offsets = (2, -1, 1, 0)

    def tree(w, h):
        t = 2 * w + h
        first, second = h, 1 - h
        r0 = h * 128

        def block(o1, o2, part=None):
            j = dp_of(first, o1, o2)
            if part is None:
                return terms.at[w, j, pl.ds(r0, 128)]
            return terms.at[w, j, pl.ds(r0 + 64 * part, 64)]

        def push(k, src, dst, axis, by):
            go(remote(src, dst, tree_send.at[t * SEMS + k], tree_recv.at[t * SEMS + k], {"dp": dp_at(axis, by)}))

        def landed(k, dst, axis, by):
            remote(dst, dst, tree_send.at[t * SEMS + k], tree_recv.at[t * SEMS + k],
                   {"dp": dp_at(axis, by)}).wait_recv()

        def s1(k):
            def event():
                push(4 * k, block(offsets[k], 2, 0), half1.at[t, k, 0], second, 1)
                push(4 * k + 1, block(offsets[k], 2, 1), half1.at[t, k, 1], second, -1)
            return event

        def s2(k):
            def event():
                landed(4 * k, half1.at[t, k, 0], second, 1)
                add_to(block(offsets[k], 1, 0), half1.at[t, k, 0])
                push(4 * k + 2, block(offsets[k], 1), full1.at[t, k, 0], second, 1)
                landed(4 * k + 1, half1.at[t, k, 1], second, -1)
                add_to(block(offsets[k], -1, 1), half1.at[t, k, 1])
                push(4 * k + 3, block(offsets[k], -1), full1.at[t, k, 1], second, -1)
            return event

        def s3(k):
            def event():
                landed(4 * k + 2, full1.at[t, k, 0], second, 1)
                landed(4 * k + 3, full1.at[t, k, 1], second, -1)
                add_to(block(offsets[k], 0), full1.at[t, k, 0], full1.at[t, k, 1])
            return event

        def s4():
            push(16, block(2, 0, 0), half2.at[t, 0], first, 1)
            push(17, block(2, 0, 1), half2.at[t, 1], first, -1)

        def s5():
            landed(16, half2.at[t, 0], first, 1)
            add_to(block(1, 0, 0), half2.at[t, 0])
            push(18, block(1, 0), full2.at[t, 0], first, 1)
            landed(17, half2.at[t, 1], first, -1)
            add_to(block(-1, 0, 1), half2.at[t, 1])
            push(19, block(-1, 0), full2.at[t, 1], first, -1)

        def s6():
            landed(18, full2.at[t, 0], first, 1)
            landed(19, full2.at[t, 1], first, -1)
            value = (block(0, 0)[...].astype(jnp.float32) + full2[t, 0].astype(jnp.float32)
                     + full2[t, 1].astype(jnp.float32))
            square[w, pl.ds(r0, 128), :] = value.astype(jnp.bfloat16)

        return [s1(0), s1(1), s1(2), s1(3)], [
            s2(0), s2(1), s2(2), s2(3), s3(0), s4, s3(1), s3(2), s5, s3(3), s6]

    def output(u, final):
        def push(k, src, dst, target):
            go(remote(src, dst, out_send.at[u * 5 + k], out_recv.at[u * 5 + k], target))

        def landed(k, dst, target):
            remote(dst, dst, out_send.at[u * 5 + k], out_recv.at[u * 5 + k], target).wait_recv()

        ahead, behind = {"enc": enc_at(1)}, {"enc": enc_at(-1)}
        top, bottom = pl.ds(0, 128), pl.ds(128, 128)

        def block(by, part=None):
            if part is None:
                return outs.at[u, core, around(py, by)]
            return outs.at[u, core, around(py, by), (top, bottom)[part]]

        def p0():
            push(0, outs.at[u, 1 - core], pair_got.at[u], sibling)

        def p1():
            landed(0, pair_got.at[u], sibling)
            add_to(block(2), pair_got.at[u, around(py, 2)])
            push(1, block(2, 0), ring_half.at[u, 0], ahead)
            push(2, block(2, 1), ring_half.at[u, 1], behind)
            for by in (1, -1, 0):
                add_to(block(by), pair_got.at[u, around(py, by)])

        def p2():
            landed(1, ring_half.at[u, 0], ahead)
            add_to(block(1, 0), ring_half.at[u, 0])
            push(3, block(1), ring_full.at[u, 0], ahead)
            landed(2, ring_half.at[u, 1], behind)
            add_to(block(-1, 1), ring_half.at[u, 1])
            push(4, block(-1), ring_full.at[u, 1], behind)

        def p3():
            landed(3, ring_full.at[u, 0], ahead)
            landed(4, ring_full.at[u, 1], behind)
            value = (block(0)[...].astype(jnp.float32) + ring_full[u, 0].astype(jnp.float32)
                     + ring_full[u, 1].astype(jnp.float32))
            final[...] = value.astype(jnp.bfloat16)

        return [p0, p1, p2, p3]

    outs0, outs1 = output(0, wide.at[0]), output(1, wide.at[1])
    lists = {w: (tree(w, 0), tree(w, 1)) for w in (3, 2, 1, 0)}

    def begin(w):
        for k in range(4):
            lists[w][0][0][k]()
            lists[w][1][0][k]()

    def then(w, lo, hi):
        for k in range(lo, hi):
            lists[w][0][1][k]()
            lists[w][1][1][k]()

    loads["small"].wait()
    loads["cot"].wait()
    fill(3, lhs.at[2], cot)
    begin(3)
    loads["wo"].wait()
    fill_out(0, lhs.at[0], wo, False)
    outs0[0]()
    loads["x"].wait()
    loads["dvt"].wait()
    fill(2, dvt, x)
    begin(2)
    then(3, 0, 4)
    loads["dkt"].wait()
    fill(1, dkt, x)
    begin(1)
    outs0[1]()
    loads["tok"].wait()
    fill(0, lhs.at[3], tok)
    begin(0)
    loads["wq"].wait()
    fill_out(1, lhs.at[1], wq, True)
    outs1[0]()
    then(2, 0, 4)
    outs0[2]()
    outs1[1]()
    then(3, 4, 8)
    then(1, 0, 4)
    then(0, 0, 4)
    outs1[2]()
    outs0[3]()
    then(3, 8, 10)
    then(2, 4, 8)
    then(1, 4, 8)
    then(2, 8, 10)
    then(0, 4, 8)
    outs1[3]()
    then(1, 8, 10)
    then(3, 10, 11)
    then(0, 8, 10)
    then(2, 10, 11)
    then(1, 10, 11)
    then(0, 10, 11)
    for copy in sends:
        copy.wait_send()


def reduce_all(small, dkt, dvt, rows_in, tokens, cotangent, wq, wo):
    bf = jnp.bfloat16
    return pl.pallas_call(
        reduce_kernel,
        out_shape=(jax.ShapeDtypeStruct((2, 256, 512), bf), jax.ShapeDtypeStruct((4, 256, 256), bf)),
        in_specs=[ANY] * 8,
        out_specs=(VMEM,) * 2,
        scratch_shapes=[
            pltpu.VMEM((1024, 4096), bf),
            pltpu.VMEM((256, 4096), bf),
            pltpu.VMEM((256, 4096), bf),
            pltpu.VMEM((16, 256, 256), bf),
            pltpu.VMEM((16, 256, 256), bf),
            pltpu.VMEM((4, 256, 256), bf),
            pltpu.VMEM((256, 1024), bf),
            pltpu.VMEM((256, 1024), bf),
            pltpu.VMEM((4, 16, 256, 256), bf),
            pltpu.VMEM((2, 2, 4, 256, 512), bf),
            pltpu.VMEM((TREES, 4, 2, 64, 256), bf),
            pltpu.VMEM((TREES, 4, 2, 128, 256), bf),
            pltpu.VMEM((TREES, 2, 64, 256), bf),
            pltpu.VMEM((TREES, 2, 128, 256), bf),
            pltpu.VMEM((2, 4, 256, 512), bf),
            pltpu.VMEM((2, 2, 128, 512), bf),
            pltpu.VMEM((2, 2, 256, 512), bf),
            pltpu.SemaphoreType.DMA((8,)),
            pltpu.SemaphoreType.DMA((TREES * SEMS,)),
            pltpu.SemaphoreType.DMA((TREES * SEMS,)),
            pltpu.SemaphoreType.DMA((10,)),
            pltpu.SemaphoreType.DMA((10,)),
        ],
        compiler_params=pltpu.CompilerParams(
            collective_id=1, has_side_effects=True, vmem_limit_bytes=56 * 1024 * 1024),
        name="reduce_all",
    )(small, dkt, dvt, rows_in, tokens, cotangent, wq, wo)


def finish_kernel(wide, square, cca, gtok, gq, gk, gv, go_out):
    cca[...] = wide[0]
    gtok[...] = wide[1]
    for w, out in ((0, gq), (1, gk), (2, gv)):
        out[...] = square[w].astype(jnp.float32).T.astype(jnp.bfloat16)
    go_out[...] = square[3]


def finish(wide, square):
    bf = jnp.bfloat16
    return pl.pallas_call(
        finish_kernel,
        out_shape=(jax.ShapeDtypeStruct((256, 512), bf),) * 2 + (jax.ShapeDtypeStruct((256, 256), bf),) * 4,
        in_specs=[VMEM] * 2,
        out_specs=(VMEM,) * 6,
        name="finish",
    )(wide, square)


def body(tokens, store, holder, rows, wq, wk, wv, wo, cotangent):
    keyrows, small, dkt, dvt, wq_all, wo_all = gather_all(holder, rows, store, wk, wv, wq, wo, tokens, cotangent)
    wide, square = reduce_all(small, dkt, dvt, keyrows.reshape(1024, 4096), tokens, cotangent, wq_all, wo_all)
    return finish(wide, square)


def solution(mesh):
    placed = (
        P("dp", None), P(("dp", "enc"), None, None), P("dp", None), P("dp"),
        P("dp", "enc"), P("dp", "enc"), P("dp", "enc"), P("enc", "dp"), P("dp", None),
    )
    return jax.shard_map(
        body, mesh=mesh, in_specs=placed,
        out_specs=(P("dp", "enc"),) * 5 + (P("enc", "dp"),),
        check_vma=False,
    )
```

```python
import functools
import math

import jax
import jax.numpy as jnp
from jax import lax
from jax.experimental import pallas as pl
from jax.experimental.pallas import tpu as pltpu
from jax.sharding import PartitionSpec as P

ANY = pl.BlockSpec(memory_space=pl.ANY)
VMEM = pl.BlockSpec(memory_space=pltpu.VMEM)
SMEM = pl.BlockSpec(memory_space=pltpu.SMEM)
HD = 128
CAP = 3
UNITS = 18
STAGES = 6
TREE_SPAN = 18
TREES = 8
SUM_SEMS = 10
TREE_SEMS = 7
NT = (((1,), (1,)), ((), ()))
TN = (((0,), (0,)), ((), ()))


def place():
    dp = lax.axis_index("dp")
    enc = lax.axis_index("enc")
    return dp // 4, dp % 4, enc // 2, enc % 2


def around(value, by):
    return lax.rem(value + (4 + by), 4)


def remote(src, dst, send, recv, target):
    return pltpu.make_async_remote_copy(
        src_ref=src, dst_ref=dst, send_sem=send, recv_sem=recv,
        device_id=target, device_id_type=pl.DeviceIdType.MESH,
    )


def count_if(flag):
    return jnp.where(flag, 1, 0)


def routes(holder, rows, y, core):
    owner = [holder[n, 0] for n in range(8)]
    row = [rows[n] for n in range(8)]
    chip = [o // 2 for o in owner]
    here = [c == y for c in chip]
    rank, chip_rank = [], []
    for n in range(8):
        a, b = jnp.int32(0), jnp.int32(0)
        for m in range(n):
            a += count_if(owner[m] == owner[n])
            b += count_if(chip[m] == chip[n])
        rank.append(a)
        chip_rank.append(b)
    picks = []
    for k in range(CAP):
        value = jnp.int32(0)
        for n in range(8):
            value += jnp.where(jnp.logical_and(owner[n] == y * 2 + core, rank[n] == k), row[n], 0)
        picks.append(value)
    capped = [jnp.minimum(r, CAP - 1) for r in rank]
    own_index = [jnp.where(owner[n] % 2 == core, capped[n], CAP + capped[n]) for n in range(8)]
    order = []
    for t in range(2 * CAP):
        value = jnp.int32(0)
        for n in range(8):
            value += jnp.where(jnp.logical_and(here[n], chip_rank[n] == t), own_index[n], 0)
        order.append(value)

    def held(c):
        value = jnp.int32(0)
        for n in range(8):
            value += count_if(chip[n] == c)
        return value

    n_here = held(y)
    spots = []
    for sign in (1, -1):
        near = 2 * jnp.maximum(held(around(y, -sign)), 1)
        mid = 2 * jnp.maximum(held(around(y, -2 * sign)), 1)
        spot = []
        for n in range(8):
            hops = lax.rem((y - chip[n]) * sign + 4, 4)
            at = 2 * chip_rank[n] + jnp.where(hops > 1, near, 0) + jnp.where(hops > 2, mid, 0)
            spot.append(jnp.minimum(at, UNITS - 2))
        spots.append(spot)
    return picks, order, n_here, here, own_index, spots


def add_to(dst, *parts):
    value = dst[...].astype(jnp.float32)
    for part in parts:
        value += part[...].astype(jnp.float32)
    dst[...] = value.astype(jnp.bfloat16)


def layer_kernel(holder, rows_in, store, wk, wv, wq, wo, tok_in, cot_in,
                 wide, square,
                 x, own_first, own_second, own_far, got, staged, weights, tok, cot,
                 kown_near, kown_far, kgot, vown_near, vown_far, vgot, q, k, v, dm, probs, small, dkt, dvt,
                 outs, half_a, full_a, half_b, full_b, half2_a, full2_a, half2_b, full2_b,
                 pair_got, ring_half, ring_full,
                 load_sem, tree_send, tree_recv, ring_send, ring_recv, pair_send, pair_recv,
                 own_send, own_recv, sum_send, sum_recv, out_send, out_recv):
    f32, bf = jnp.float32, jnp.bfloat16
    px, pz, y, core = place()
    dp = px * 4 + pz
    sources = (wk, wv, wq, wo)
    own_near = (own_first, own_second)

    def dp_at(axis, by):
        if axis == 0:
            return around(px, by) * 4 + pz
        return px * 4 + around(pz, by)

    def dp_of(first, o1, o2):
        if first == 0:
            return around(px, o1) * 4 + around(pz, o2)
        return around(px, o2) * 4 + around(pz, o1)

    def enc_at(by):
        return around(y, by) * 2 + core

    sibling = {"enc": y * 2 + 1 - core}
    load_store = pltpu.make_async_copy(store, x, load_sem.at[0])
    load_store.start()
    keeps = []
    for i in range(4):
        copy = pltpu.make_async_copy(sources[i], weights.at[i, dp], load_sem.at[1 + i])
        copy.start()
        keeps.append(copy)
    load_tok = pltpu.make_async_copy(tok_in, tok, load_sem.at[5])
    load_cot = pltpu.make_async_copy(cot_in, cot, load_sem.at[6])

    barrier = pltpu.get_barrier_semaphore()
    peers = ([{"dp": dp_at(a, b)} for a in (0, 1) for b in (1, -1)]
             + [{"enc": enc_at(1)}, {"enc": enc_at(-1)}, sibling])
    for peer in peers:
        pl.semaphore_signal(barrier, inc=1, device_id=peer, device_id_type=pl.DeviceIdType.MESH)
    picks, order, n_here, here, own_index, spots = routes(holder, rows_in, y, core)
    lag = 2 * jnp.maximum(n_here, 1)
    load_store.wait()

    def lane(of, way, r):
        return pl.ds(of * 64 + way * 32 + r * 16, 16)

    for r in (0, 1):
        for i in range(CAP):
            for way in (0, 1):
                own_far[r, i, way] = x[picks[i], lane(1 - core, way, r)]
                own_near[r][i, way] = x[picks[i], lane(core, way, r)]
    pl.semaphore_wait(barrier, len(peers))

    def slot(w, j, part=None):
        if part is None:
            return weights.at[w, j]
        return weights.at[w, j, pl.ds(part * 128, 128)]

    def push(w, group, src, dst, axis, by):
        remote(src, dst, tree_send.at[w], tree_recv.at[w, group], {"dp": dp_at(axis, by)}).start()

    def landed(w, group, pieces):
        ref = weights.at[w, pl.ds(0, pieces)]
        remote(ref, ref, tree_send.at[w], tree_recv.at[w, group], {"dp": dp_at(0, 1)}).wait_recv()

    def tree_sent(w):
        ref = weights.at[w, pl.ds(0, 15)]
        remote(ref, ref, tree_send.at[w], tree_recv.at[w, 0], {"dp": dp_at(0, 1)}).wait_send()

    offsets = (0, -1, 1, 2)

    def tree_events(w):
        first = w % 2
        second = 1 - first
        own_block = sources[w]

        def spread(i, src, j):
            push(w, 2 + i, src, slot(w, j), second, 1)
            push(w, 2 + i, src, slot(w, j), second, -1)

        def e0():
            push(w, 0, own_block, slot(w, dp), first, 1)
            push(w, 0, own_block, slot(w, dp), first, -1)

        def e1():
            spread(0, own_block, dp)

        def e2():
            landed(w, 0, 2)
            behind, ahead = dp_of(first, -1, 0), dp_of(first, 1, 0)
            push(w, 1, slot(w, behind, 0), slot(w, behind, 0), first, 1)
            push(w, 1, slot(w, ahead, 1), slot(w, ahead, 1), first, -1)
            spread(1, slot(w, behind), behind)
            spread(2, slot(w, ahead), ahead)

        def e3():
            landed(w, 1, 1)
            j = dp_of(first, 2, 0)
            spread(3, slot(w, j), j)

        def forward(i):
            def event():
                landed(w, 2 + i, 2)
                j = dp_of(first, offsets[i], -1)
                push(w, 6, slot(w, j, 0), slot(w, j, 0), second, 1)
                j = dp_of(first, offsets[i], 1)
                push(w, 6, slot(w, j, 1), slot(w, j, 1), second, -1)
            return event

        def last():
            landed(w, 6, 4)

        return [e0, e1, e2, forward(0), e3, forward(1), forward(2), forward(3), last]

    per = [tree_events(w) for w in range(4)]
    queue = []
    ends = {}
    for pair in ((0, 1), (2, 3)):
        for i in range(9):
            for w in pair:
                queue.append((i + 6 * (w // 2), w, i))
    queue.sort()
    for w in range(4):
        ends[w] = queue.index((8 + 6 * (w // 2), w, 8)) + 1
    queue = [per[w][i] for _, w, i in queue]
    total = len(queue)
    done = [0]

    def advance(upto):
        while done[0] < min(upto, total):
            queue[done[0]]()
            done[0] += 1

    swaps = [remote(own_far.at[r, pl.ds(0, CAP)], own_near[r].at[pl.ds(CAP, CAP)], own_send.at[r], own_recv.at[r], sibling)
             for r in (0, 1)]
    backs = [remote(own_near[r].at[pl.ds(0, CAP)], own_far.at[r, pl.ds(CAP, CAP)], own_send.at[2 + r], own_recv.at[2 + r], sibling)
             for r in (0, 1)]
    swaps[0].start()
    advance(2)
    swaps[1].start()
    load_tok.start()
    load_cot.start()
    advance(4)

    groups = ((0, 4), (4, 8), (8, 12), (12, 15), (15, 18))
    group_of = [i for i, (lo, hi) in enumerate(groups) for _ in range(lo, hi)]

    def pair_wait(group):
        lo, hi = groups[group]
        ref = got.at[pl.ds(lo, hi - lo), pl.ds(2 * (1 - core), 2)]
        remote(ref, ref, pair_send, pair_recv.at[group], sibling).wait_recv()

    def project(w, value):
        return jnp.dot(value, weights[w].reshape(4096, 256), preferred_element_type=f32).astype(bf)

    def kv_near():
        advance(ends[1])
        for copy in keeps[:2]:
            copy.wait()
        for r in (0, 1):
            value = own_near[r][...].reshape(192, 4096)
            kown_near[r] = project(0, value).reshape(6, 2, 16, 256)
            vown_near[r] = project(1, value).reshape(6, 2, 16, 256)

    def kv_far():
        for copy in backs:
            copy.wait_recv()
        value = own_far[...].reshape(384, 4096)
        kown_far[...] = project(0, value).reshape(2, 6, 2, 16, 256)
        vown_far[...] = project(1, value).reshape(2, 6, 2, 16, 256)

    def kv_got(group):
        def event():
            lo, hi = groups[group]
            pair_wait(group)
            value = got[lo:hi].reshape((hi - lo) * 64, 4096)
            kgot[lo:hi] = project(0, value).reshape(hi - lo, 4, 16, 256)
            vgot[lo:hi] = project(1, value).reshape(hi - lo, 4, 16, 256)
        return event

    def queries():
        advance(ends[2])
        keeps[2].wait()
        load_tok.wait()
        q[...] = project(2, tok[...])

    def upstream():
        advance(ends[3])
        keeps[3].wait()
        load_cot.wait()
        acc = jnp.zeros((256, 256), f32)
        for j in range(16):
            acc += lax.dot_general(cot[:, 256 * j:256 * j + 256], weights[3, j], NT, preferred_element_type=f32)
        dm[...] = acc.astype(bf)

    def ring_ref(u):
        return got.at[u, pl.ds(2 * core, 2)]

    def staged_sent(u):
        ref = staged.at[u % STAGES]
        remote(ref, ref, ring_send.at[u % STAGES], ring_recv.at[u], sibling).wait_send()

    work = {11: kv_near, 12: kv_far, 13: kv_got(0), 14: kv_got(1), 15: queries, 16: kv_got(2),
            18: upstream, 19: kv_got(3)}
    for u in range(UNITS + 2):
        if u >= 2:
            remote(ring_ref(u - 2), ring_ref(u - 2), ring_send.at[0], ring_recv.at[u - 2], sibling).wait_recv()
        if u < UNITS:
            if u < 2:
                swaps[u].wait_recv()
            if u >= STAGES:
                staged_sent(u - STAGES)
            for way in (0, 1):
                value = own_near[u % 2][order[min(u // 2, 5)], way]
                for back in (2, 4, 6, 8, 10, 12):
                    if u - back >= 0:
                        use = jnp.logical_and(2 * n_here <= u, lag == back)
                        value = jnp.where(use, got[u - back, 2 * core + way], value)
                staged[u % STAGES, way] = value
                remote(staged.at[u % STAGES, way], got.at[u, 2 * core + way],
                       ring_send.at[u % STAGES], ring_recv.at[u], {"enc": enc_at(1 - 2 * way)}).start()
        if u >= 2:
            remote(ring_ref(u - 2), ring_ref(u - 2), pair_send, pair_recv.at[group_of[u - 2]], sibling).start()
        if u in (2, 3):
            backs[u - 2].start()
        advance(4 + (total - 4) * (u + 1) // TREE_SPAN)
        if u in work:
            work[u]()
    advance(total)
    kv_got(4)()

    def key_rows(n, way, r, of, own, pool):
        return jnp.where(here[n], own, pool[spots[way][n] + r, 2 * of + way])

    for n in range(8):
        for way in (0, 1):
            for r in (0, 1):
                at = pl.ds((n % 2) * 128 + core * 64 + way * 32 + r * 16, 16)
                k[n // 2, at] = key_rows(n, way, r, core, kown_near[r, own_index[n], way], kgot)
                v[n // 2, at] = key_rows(n, way, r, core, vown_near[r, own_index[n], way], vgot)
                at = pl.ds((n % 2) * 128 + (1 - core) * 64 + way * 32 + r * 16, 16)
                k[n // 2, at] = key_rows(n, way, r, 1 - core, kown_far[r, own_index[n], way], kgot)
                v[n // 2, at] = key_rows(n, way, r, 1 - core, vown_far[r, own_index[n], way], vgot)

    def order_rows():
        for n in range(8):
            for way in (0, 1):
                for r in (0, 1):
                    x[n, lane(core, way, r)] = key_rows(n, way, r, core, own_near[r][own_index[n], way], got)
                    x[n, lane(1 - core, way, r)] = key_rows(n, way, r, 1 - core, own_far[r, own_index[n], way], got)

    scale = 1.0 / math.sqrt(HD)
    pairs = [(c, h, slice(64 * c, 64 * c + 64), slice(128 * h, 128 * h + 128)) for c in range(4) for h in range(2)]
    for c, h, t, e in pairs:
        s = lax.dot_general(q[t, e], k[c, :, e], NT, preferred_element_type=f32) * scale
        p = jnp.exp(s - jnp.max(s, axis=-1, keepdims=True))
        p = p / jnp.sum(p, axis=-1, keepdims=True)
        probs[c, h] = p
        small[0, t, e] = jnp.dot(p.astype(bf), v[c, :, e], preferred_element_type=f32).astype(bf)
    small[2] = small[0].astype(f32).T.astype(bf)

    def backward():
        for c, h, t, e in pairs:
            p = probs[c, h]
            dprob = lax.dot_general(dm[t, e], v[c, :, e], NT, preferred_element_type=f32)
            ds = (p * (dprob - jnp.sum(dprob * p, axis=-1, keepdims=True)) * scale).astype(bf)
            small[1, t, e] = jnp.dot(ds, k[c, :, e], preferred_element_type=f32).astype(bf)
            dkt[e, 256 * c:256 * c + 256] = lax.dot_general(q[t, e], ds, TN, preferred_element_type=f32).astype(bf)
            dvt[e, 256 * c:256 * c + 256] = lax.dot_general(dm[t, e], p.astype(bf), TN, preferred_element_type=f32).astype(bf)
        small[3] = small[1].astype(f32).T.astype(bf)

    def fill_flat(place_of, left, right):
        def step(j, carry):
            cols = pl.ds(pl.multiple_of(j * 256, 256), 256)
            weights[place_of, j] = jnp.dot(left[...], right[:, cols], preferred_element_type=f32).astype(bf)
            return carry
        lax.fori_loop(0, 16, step, 0)

    def fill_rows(place_of, left):
        def step(j, carry):
            cols = pl.ds(pl.multiple_of(j * 256, 256), 256)
            value = jnp.dot(left[...], x[:, :, cols].reshape(1024, 256), preferred_element_type=f32).astype(bf)
            got[4 * place_of:4 * place_of + 4, :, :, cols] = value.reshape(4, 4, 16, 256)
            return carry
        lax.fori_loop(0, 16, step, 0)

    def fill_out(u, left, w, flip):
        dims = (((1,), (1 if flip else 0,)), ((), ()))

        def step(j, carry):
            e = j // 2
            value = lax.dot_general(left[...], weights[w, j], dims, preferred_element_type=f32)
            cols = pl.ds(pl.multiple_of((j % 2) * 256, 256), 256)
            outs[u, e % 2, e // 2, :, cols] = value.astype(bf)
            return carry
        lax.fori_loop(0, 16, step, 0)

    ranks = (2, -1, 1, 0)

    def sum_tree(w, h):
        t = 2 * w + h
        first, second = h, 1 - h
        flat = w in (0, 3)
        if flat:
            b = 2 * (w == 0) + h
            half1, full1, half2, full2 = half_a.at[b], full_a.at[b], half2_a.at[b], full2_a.at[b]
        else:
            b = 2 * (w == 1) + h
            half1, full1, half2, full2 = half_b.at[b], full_b.at[b], half2_b.at[b], full2_b.at[b]

        def block(o1, o2, part=None):
            j = dp_of(first, o1, o2)
            if flat:
                if part is None:
                    return weights.at[int(w == 0), j, pl.ds(128 * h, 128)]
                return weights.at[int(w == 0), j, pl.ds(128 * h + 64 * part, 64)]
            cols = pl.ds(pl.multiple_of(j * 256, 256), 256)
            if part is None:
                return got.at[pl.ds(2 * b, 2), :, :, cols]
            return got.at[2 * b + part, :, :, cols]

        def push(group, src, dst, axis, by):
            remote(src, dst, sum_send.at[t], sum_recv.at[t, group], {"dp": dp_at(axis, by)}).start()

        def landed(group, ref):
            remote(ref, ref, sum_send.at[t], sum_recv.at[t, group], {"dp": dp_at(0, 1)}).wait_recv()

        def s1(i):
            def event():
                push(i, block(ranks[i], 2, 0), half1.at[i, 0], second, 1)
                push(i, block(ranks[i], 2, 1), half1.at[i, 1], second, -1)
            return event

        def s2(i):
            def event():
                landed(i, half1.at[i])
                add_to(block(ranks[i], 1, 0), half1.at[i, 0])
                push(4 + i, block(ranks[i], 1), full1.at[i, 0], second, 1)
                add_to(block(ranks[i], -1, 1), half1.at[i, 1])
                push(4 + i, block(ranks[i], -1), full1.at[i, 1], second, -1)
            return event

        def s3(i):
            def event():
                landed(4 + i, full1.at[i])
                add_to(block(ranks[i], 0), full1.at[i, 0], full1.at[i, 1])
            return event

        def s4():
            push(8, block(2, 0, 0), half2.at[0], first, 1)
            push(8, block(2, 0, 1), half2.at[1], first, -1)

        def s5():
            landed(8, half2)
            add_to(block(1, 0, 0), half2.at[0])
            push(9, block(1, 0), full2.at[0], first, 1)
            add_to(block(-1, 0, 1), half2.at[1])
            push(9, block(-1, 0), full2.at[1], first, -1)

        def s6():
            landed(9, full2)
            value = block(0, 0)[...].astype(f32) + full2[0].astype(f32) + full2[1].astype(f32)
            square[w, pl.ds(128 * h, 128), :] = value.astype(bf).reshape(128, 256)

        return [s1(0), s1(1), s1(2), s1(3)], [
            s2(0), s2(1), s2(2), s2(3), s3(0), s4, s3(1), s3(2), s5, s3(3), s6]

    def output(u, final):
        def push(group, src, dst, target):
            remote(src, dst, out_send.at[u, group], out_recv.at[u, group], target).start()

        def landed(group, ref):
            remote(ref, ref, out_send.at[u, group], out_recv.at[u, group], sibling).wait_recv()

        ahead, behind = {"enc": enc_at(1)}, {"enc": enc_at(-1)}
        top, bottom = pl.ds(0, 128), pl.ds(128, 128)

        def block(by, part=None):
            if part is None:
                return outs.at[u, core, around(y, by)]
            return outs.at[u, core, around(y, by), (top, bottom)[part]]

        def p0():
            push(0, outs.at[u, 1 - core], pair_got.at[u], sibling)

        def p1():
            landed(0, pair_got.at[u])
            add_to(block(2), pair_got.at[u, around(y, 2)])
            push(1, block(2, 0), ring_half.at[u, 0], ahead)
            push(1, block(2, 1), ring_half.at[u, 1], behind)
            for by in (1, -1, 0):
                add_to(block(by), pair_got.at[u, around(y, by)])

        def p2():
            landed(1, ring_half.at[u])
            add_to(block(1, 0), ring_half.at[u, 0])
            push(2, block(1), ring_full.at[u, 0], ahead)
            add_to(block(-1, 1), ring_half.at[u, 1])
            push(2, block(-1), ring_full.at[u, 1], behind)

        def p3():
            landed(2, ring_full.at[u])
            value = (block(0)[...].astype(jnp.float32) + ring_full[u, 0].astype(jnp.float32)
                     + ring_full[u, 1].astype(jnp.float32))
            final[...] = value.astype(jnp.bfloat16)

        return [p0, p1, p2, p3]

    outs0, outs1 = output(0, wide.at[0]), output(1, wide.at[1])
    lists = {w: (sum_tree(w, 0), sum_tree(w, 1)) for w in (3, 2, 1, 0)}

    def begin(w):
        for k in range(4):
            lists[w][0][0][k]()
            lists[w][1][0][k]()

    def then(w, lo, hi):
        for k in range(lo, hi):
            lists[w][0][1][k]()
            lists[w][1][1][k]()

    for w in range(4):
        tree_sent(w)
    for u in range(UNITS - STAGES, UNITS):
        staged_sent(u)
    remote(got.at[:, pl.ds(0, 2)], got.at[:, pl.ds(0, 2)], pair_send, pair_recv.at[0], sibling).wait_send()
    for copy in swaps + backs:
        copy.wait_send()
    fill_flat(0, small.at[2], cot)
    begin(3)
    fill_out(0, small.at[0], 3, False)
    outs0[0]()
    backward()
    fill_flat(1, small.at[3], tok)
    begin(0)
    then(3, 0, 4)
    order_rows()
    fill_rows(0, dvt)
    begin(2)
    then(0, 0, 4)
    outs0[1]()
    fill_rows(1, dkt)
    begin(1)
    then(3, 4, 8)
    fill_out(1, small.at[1], 2, True)
    outs1[0]()
    then(2, 0, 4)
    outs0[2]()
    then(0, 4, 8)
    then(1, 0, 4)
    outs1[1]()
    then(3, 8, 10)
    outs0[3]()
    then(2, 4, 8)
    outs1[2]()
    then(0, 8, 10)
    then(1, 4, 8)
    then(3, 10, 11)
    then(2, 8, 10)
    outs1[3]()
    then(0, 10, 11)
    then(1, 8, 10)
    then(2, 10, 11)
    then(1, 10, 11)
    for t in range(TREES):
        ref = weights.at[3, pl.ds(0, 15), pl.ds(0, 128)]
        remote(ref, ref, sum_send.at[t], sum_recv.at[t, 0], sibling).wait_send()
    for u in (0, 1):
        for group, ref in enumerate((pair_got.at[u], ring_half.at[u], ring_full.at[u])):
            remote(ref, ref, out_send.at[u, group], out_recv.at[u, group], sibling).wait_send()


def layer(holder, rows, store, wk, wv, wq, wo, tokens, cotangent):
    bf = jnp.bfloat16
    dma = pltpu.SemaphoreType.DMA
    vm = pltpu.VMEM
    return pl.pallas_call(
        layer_kernel,
        out_shape=(jax.ShapeDtypeStruct((2, 256, 512), bf), jax.ShapeDtypeStruct((4, 256, 256), bf)),
        in_specs=[SMEM, SMEM] + [ANY] * 7,
        out_specs=(VMEM, VMEM),
        scratch_shapes=[
            vm((8, 128, 4096), bf),
            vm((2 * CAP, 2, 16, 4096), bf),
            vm((2 * CAP, 2, 16, 4096), bf),
            vm((2, 2 * CAP, 2, 16, 4096), bf),
            vm((UNITS, 4, 16, 4096), bf),
            vm((STAGES, 2, 16, 4096), bf),
            vm((4, 16, 256, 256), bf),
            vm((256, 4096), bf),
            vm((256, 4096), bf),
            vm((2, 2 * CAP, 2, 16, 256), bf),
            vm((2, 2 * CAP, 2, 16, 256), bf),
            vm((UNITS, 4, 16, 256), bf),
            vm((2, 2 * CAP, 2, 16, 256), bf),
            vm((2, 2 * CAP, 2, 16, 256), bf),
            vm((UNITS, 4, 16, 256), bf),
            vm((256, 256), bf),
            vm((4, 256, 256), bf),
            vm((4, 256, 256), bf),
            vm((256, 256), bf),
            vm((4, 2, 64, 256), jnp.float32),
            vm((4, 256, 256), bf),
            vm((256, 1024), bf),
            vm((256, 1024), bf),
            vm((2, 2, 4, 256, 512), bf),
            vm((4, 4, 2, 64, 256), bf),
            vm((4, 4, 2, 128, 256), bf),
            vm((4, 4, 2, 4, 16, 256), bf),
            vm((4, 4, 2, 2, 4, 16, 256), bf),
            vm((4, 2, 64, 256), bf),
            vm((4, 2, 128, 256), bf),
            vm((4, 2, 4, 16, 256), bf),
            vm((4, 2, 2, 4, 16, 256), bf),
            vm((2, 4, 256, 512), bf),
            vm((2, 2, 128, 512), bf),
            vm((2, 2, 256, 512), bf),
            dma((7,)),
            dma((4,)),
            dma((4, TREE_SEMS)),
            dma((STAGES,)),
            dma((UNITS,)),
            dma(()),
            dma((5,)),
            dma((4,)),
            dma((4,)),
            dma((TREES,)),
            dma((TREES, SUM_SEMS)),
            dma((2, 3)),
            dma((2, 3)),
        ],
        compiler_params=pltpu.CompilerParams(
            collective_id=0, has_side_effects=True, vmem_limit_bytes=62 * 1024 * 1024),
        name="layer",
    )(holder, rows, store, wk, wv, wq, wo, tokens, cotangent)


def finish_kernel(wide, square, cca, gtok, gq, gk, gv, go_out):
    cca[...] = wide[0]
    gtok[...] = wide[1]
    for w, out in ((0, gq), (1, gk), (2, gv)):
        out[...] = square[w].astype(jnp.float32).T.astype(jnp.bfloat16)
    go_out[...] = square[3]


def finish(wide, square):
    bf = jnp.bfloat16
    return pl.pallas_call(
        finish_kernel,
        out_shape=(jax.ShapeDtypeStruct((256, 512), bf),) * 2 + (jax.ShapeDtypeStruct((256, 256), bf),) * 4,
        in_specs=[VMEM] * 2,
        out_specs=(VMEM,) * 6,
        name="finish",
    )(wide, square)


def body(tokens, store, holder, rows, wq, wk, wv, wo, cotangent):
    return finish(*layer(holder, rows, store, wk, wv, wq, wo, tokens, cotangent))


def solution(mesh):
    placed = (
        P("dp", None), P(("dp", "enc"), None, None), P("dp", None), P("dp"),
        P("dp", "enc"), P("dp", "enc"), P("dp", "enc"), P("enc", "dp"), P("dp", None),
    )
    return jax.shard_map(
        body, mesh=mesh, in_specs=placed,
        out_specs=(P("dp", "enc"),) * 5 + (P("enc", "dp"),),
        check_vma=False,
    )
```

```python
import functools
import math

import jax
import jax.numpy as jnp
from jax import lax
from jax.experimental import pallas as pl
from jax.experimental.pallas import tpu as pltpu
from jax.sharding import PartitionSpec as P

ANY = pl.BlockSpec(memory_space=pl.ANY)
VMEM = pl.BlockSpec(memory_space=pltpu.VMEM)
SMEM = pl.BlockSpec(memory_space=pltpu.SMEM)
HD = 128
CAP = 3
UNITS = 18
STAGES = 6
TREE_SPAN = 18
UNROLL = 1
TREES = 8
SUM_SEMS = 10
TREE_SEMS = 7
NT = (((1,), (1,)), ((), ()))
TN = (((0,), (0,)), ((), ()))


def place():
    dp = lax.axis_index("dp")
    enc = lax.axis_index("enc")
    return dp // 4, dp % 4, enc // 2, enc % 2


def around(value, by):
    return lax.rem(value + (4 + by), 4)


def remote(src, dst, send, recv, target):
    return pltpu.make_async_remote_copy(
        src_ref=src, dst_ref=dst, send_sem=send, recv_sem=recv,
        device_id=target, device_id_type=pl.DeviceIdType.MESH,
    )


def count_if(flag):
    return jnp.where(flag, 1, 0)


def routes(holder, rows, y, core):
    owner = [holder[n] for n in range(8)]
    row = [rows[n] for n in range(8)]
    chip = [o // 2 for o in owner]
    here = [c == y for c in chip]
    rank, chip_rank = [], []
    for n in range(8):
        a, b = jnp.int32(0), jnp.int32(0)
        for m in range(n):
            a += count_if(owner[m] == owner[n])
            b += count_if(chip[m] == chip[n])
        rank.append(a)
        chip_rank.append(b)
    picks = []
    for k in range(CAP):
        value = jnp.int32(0)
        for n in range(8):
            value += jnp.where(jnp.logical_and(owner[n] == y * 2 + core, rank[n] == k), row[n], 0)
        picks.append(value)
    capped = [jnp.minimum(r, CAP - 1) for r in rank]
    own_index = [jnp.where(owner[n] % 2 == core, capped[n], CAP + capped[n]) for n in range(8)]
    order = []
    for t in range(2 * CAP):
        value = jnp.int32(0)
        for n in range(8):
            value += jnp.where(jnp.logical_and(here[n], chip_rank[n] == t), own_index[n], 0)
        order.append(value)

    def held(c):
        value = jnp.int32(0)
        for n in range(8):
            value += count_if(chip[n] == c)
        return value

    n_here = held(y)
    spots = []
    for sign in (1, -1):
        near = 2 * jnp.maximum(held(around(y, -sign)), 1)
        mid = 2 * jnp.maximum(held(around(y, -2 * sign)), 1)
        spot = []
        for n in range(8):
            hops = lax.rem((y - chip[n]) * sign + 4, 4)
            at = 2 * chip_rank[n] + jnp.where(hops > 1, near, 0) + jnp.where(hops > 2, mid, 0)
            spot.append(jnp.minimum(at, UNITS - 2))
        spots.append(spot)
    return picks, order, n_here, here, own_index, spots


def add_to(dst, *parts):
    value = dst[...].astype(jnp.float32)
    for part in parts:
        value += part[...].astype(jnp.float32)
    dst[...] = value.astype(jnp.bfloat16)


def layer_kernel(holder, rows_in, store, wk, wv, wq, wo, tok_in, cot_in,
                 wide, square,
                 x, own_first, own_second, own_far, got, staged, weights, tok, cot,
                 kown_near, kown_far, kgot, vown_near, vown_far, vgot, q, k, v, dm, probs, dscore, small, dkt, dvt,
                 outs, half_a, full_a, half_b, full_b, half2_a, full2_a, half2_b, full2_b,
                 pair_got, ring_half, ring_full,
                 load_sem, tree_send, tree_recv, ring_send, ring_recv, pair_send, pair_recv,
                 own_send, own_recv, sum_send, sum_recv, out_send, out_recv):
    f32, bf = jnp.float32, jnp.bfloat16
    px, pz, y, core = place()
    dp = px * 4 + pz
    sources = (wk, wv, wq, wo)
    own_near = (own_first, own_second)

    def dp_at(axis, by):
        if axis == 0:
            return around(px, by) * 4 + pz
        return px * 4 + around(pz, by)

    def dp_of(first, o1, o2):
        if first == 0:
            return around(px, o1) * 4 + around(pz, o2)
        return around(px, o2) * 4 + around(pz, o1)

    def enc_at(by):
        return around(y, by) * 2 + core

    sibling = {"enc": y * 2 + 1 - core}
    load_store = pltpu.make_async_copy(store, x, load_sem.at[0])
    load_store.start()
    keeps = []
    for i in range(4):
        copy = pltpu.make_async_copy(sources[i], weights.at[i, dp], load_sem.at[1 + i])
        copy.start()
        keeps.append(copy)
    load_tok = pltpu.make_async_copy(tok_in, tok, load_sem.at[5])
    load_cot = pltpu.make_async_copy(cot_in, cot, load_sem.at[6])

    barrier = pltpu.get_barrier_semaphore()
    peers = ([{"dp": dp_at(a, b)} for a in (0, 1) for b in (1, -1)]
             + [{"enc": enc_at(1)}, {"enc": enc_at(-1)}, sibling])
    for peer in peers:
        pl.semaphore_signal(barrier, inc=1, device_id=peer, device_id_type=pl.DeviceIdType.MESH)
    picks, order, n_here, here, own_index, spots = routes(holder, rows_in, y, core)
    lag = 2 * jnp.maximum(n_here, 1)
    load_store.wait()

    def lane(of, way, r):
        return pl.ds(of * 64 + way * 32 + r * 16, 16)

    for r in (0, 1):
        for i in range(CAP):
            for way in (0, 1):
                own_far[r, i, way] = x[picks[i], lane(1 - core, way, r)]
                own_near[r][i, way] = x[picks[i], lane(core, way, r)]
    pl.semaphore_wait(barrier, len(peers))

    def slot(w, j, part=None):
        if part is None:
            return weights.at[w, j]
        return weights.at[w, j, pl.ds(part * 128, 128)]

    def push(w, group, src, dst, axis, by):
        remote(src, dst, tree_send.at[w], tree_recv.at[w, group], {"dp": dp_at(axis, by)}).start()

    def landed(w, group, pieces):
        ref = weights.at[w, pl.ds(0, pieces)]
        remote(ref, ref, tree_send.at[w], tree_recv.at[w, group], {"dp": dp_at(0, 1)}).wait_recv()

    def tree_sent(w):
        ref = weights.at[w, pl.ds(0, 15)]
        remote(ref, ref, tree_send.at[w], tree_recv.at[w, 0], {"dp": dp_at(0, 1)}).wait_send()

    offsets = (0, -1, 1, 2)

    def tree_events(w):
        first = w % 2
        second = 1 - first
        own_block = sources[w]

        def spread(i, src, j):
            push(w, 2 + i, src, slot(w, j), second, 1)
            push(w, 2 + i, src, slot(w, j), second, -1)

        def e0():
            push(w, 0, own_block, slot(w, dp), first, 1)
            push(w, 0, own_block, slot(w, dp), first, -1)

        def e1():
            spread(0, own_block, dp)

        def e2():
            landed(w, 0, 2)
            behind, ahead = dp_of(first, -1, 0), dp_of(first, 1, 0)
            push(w, 1, slot(w, behind, 0), slot(w, behind, 0), first, 1)
            push(w, 1, slot(w, ahead, 1), slot(w, ahead, 1), first, -1)
            spread(1, slot(w, behind), behind)
            spread(2, slot(w, ahead), ahead)

        def e3():
            landed(w, 1, 1)
            j = dp_of(first, 2, 0)
            spread(3, slot(w, j), j)

        def forward(i):
            def event():
                landed(w, 2 + i, 2)
                j = dp_of(first, offsets[i], -1)
                push(w, 6, slot(w, j, 0), slot(w, j, 0), second, 1)
                j = dp_of(first, offsets[i], 1)
                push(w, 6, slot(w, j, 1), slot(w, j, 1), second, -1)
            return event

        def last():
            landed(w, 6, 4)

        return [e0, e1, e2, forward(0), e3, forward(1), forward(2), forward(3), last]

    per = [tree_events(w) for w in range(4)]
    queue = []
    ends = {}
    for pair in ((0, 1), (2, 3)):
        for i in range(9):
            for w in pair:
                queue.append((i + 6 * (w // 2), w, i))
    queue.sort()
    for w in range(4):
        ends[w] = queue.index((8 + 6 * (w // 2), w, 8)) + 1
    queue = [per[w][i] for _, w, i in queue]
    total = len(queue)
    done = [0]

    def advance(upto):
        while done[0] < min(upto, total):
            queue[done[0]]()
            done[0] += 1

    swaps = [remote(own_far.at[r, pl.ds(0, CAP)], own_near[r].at[pl.ds(CAP, CAP)], own_send.at[r], own_recv.at[r], sibling)
             for r in (0, 1)]
    backs = [remote(own_near[r].at[pl.ds(0, CAP)], own_far.at[r, pl.ds(CAP, CAP)], own_send.at[2 + r], own_recv.at[2 + r], sibling)
             for r in (0, 1)]
    swaps[0].start()
    advance(2)
    swaps[1].start()
    load_tok.start()
    load_cot.start()
    advance(4)

    groups = ((0, 4), (4, 8), (8, 12), (12, 15), (15, 18))
    group_of = [i for i, (lo, hi) in enumerate(groups) for _ in range(lo, hi)]

    def pair_wait(group):
        lo, hi = groups[group]
        ref = got.at[pl.ds(lo, hi - lo), pl.ds(2 * (1 - core), 2)]
        remote(ref, ref, pair_send, pair_recv.at[group], sibling).wait_recv()

    def project(w, value):
        return jnp.dot(value, weights[w].reshape(4096, 256), preferred_element_type=f32).astype(bf)

    def kv_near():
        advance(ends[1])
        for copy in keeps[:2]:
            copy.wait()
        for r in (0, 1):
            value = own_near[r][...].reshape(192, 4096)
            kown_near[r] = project(0, value).reshape(6, 2, 16, 256)
            vown_near[r] = project(1, value).reshape(6, 2, 16, 256)

    def kv_far():
        for copy in backs:
            copy.wait_recv()
        value = own_far[...].reshape(384, 4096)
        kown_far[...] = project(0, value).reshape(2, 6, 2, 16, 256)
        vown_far[...] = project(1, value).reshape(2, 6, 2, 16, 256)

    def kv_got(group):
        def event():
            lo, hi = groups[group]
            pair_wait(group)
            value = got[lo:hi].reshape((hi - lo) * 64, 4096)
            kgot[lo:hi] = project(0, value).reshape(hi - lo, 4, 16, 256)
            vgot[lo:hi] = project(1, value).reshape(hi - lo, 4, 16, 256)
        return event

    def queries():
        advance(ends[2])
        keeps[2].wait()
        load_tok.wait()
        q[...] = project(2, tok[...])

    def upstream():
        advance(ends[3])
        keeps[3].wait()
        load_cot.wait()
        acc = jnp.zeros((256, 256), f32)
        for j in range(16):
            acc += lax.dot_general(cot[:, 256 * j:256 * j + 256], weights[3, j], NT, preferred_element_type=f32)
        dm[...] = acc.astype(bf)

    def ring_ref(u):
        return got.at[u, pl.ds(2 * core, 2)]

    def staged_sent(u):
        ref = staged.at[u % STAGES]
        remote(ref, ref, ring_send.at[u % STAGES], ring_recv.at[u], sibling).wait_send()

    work = {11: kv_near, 12: kv_far, 13: kv_got(0), 14: kv_got(1), 15: queries, 16: kv_got(2),
            18: upstream, 19: kv_got(3)}
    for u in range(UNITS + 2):
        if u >= 2:
            remote(ring_ref(u - 2), ring_ref(u - 2), ring_send.at[0], ring_recv.at[u - 2], sibling).wait_recv()
        if u < UNITS:
            if u < 2:
                swaps[u].wait_recv()
            if u >= STAGES:
                staged_sent(u - STAGES)
            for way in (0, 1):
                value = own_near[u % 2][order[min(u // 2, 5)], way]
                for back in (2, 4, 6, 8, 10, 12):
                    if u - back >= 0:
                        use = jnp.logical_and(2 * n_here <= u, lag == back)
                        value = jnp.where(use, got[u - back, 2 * core + way], value)
                staged[u % STAGES, way] = value
                remote(staged.at[u % STAGES, way], got.at[u, 2 * core + way],
                       ring_send.at[u % STAGES], ring_recv.at[u], {"enc": enc_at(1 - 2 * way)}).start()
        if u >= 2:
            remote(ring_ref(u - 2), ring_ref(u - 2), pair_send, pair_recv.at[group_of[u - 2]], sibling).start()
        if u in (2, 3):
            backs[u - 2].start()
        advance(4 + (total - 4) * (u + 1) // TREE_SPAN)
        if u in work:
            work[u]()
    advance(total)
    kv_got(4)()

    def key_rows(n, way, r, of, own, pool):
        return jnp.where(here[n], own, pool[spots[way][n] + r, 2 * of + way])

    for n in range(8):
        for way in (0, 1):
            for r in (0, 1):
                at = pl.ds((n % 2) * 128 + core * 64 + way * 32 + r * 16, 16)
                k[n // 2, at] = key_rows(n, way, r, core, kown_near[r, own_index[n], way], kgot)
                v[n // 2, at] = key_rows(n, way, r, core, vown_near[r, own_index[n], way], vgot)
                at = pl.ds((n % 2) * 128 + (1 - core) * 64 + way * 32 + r * 16, 16)
                k[n // 2, at] = key_rows(n, way, r, 1 - core, kown_far[r, own_index[n], way], kgot)
                v[n // 2, at] = key_rows(n, way, r, 1 - core, vown_far[r, own_index[n], way], vgot)

    def order_rows():
        for n in range(8):
            for way in (0, 1):
                for r in (0, 1):
                    x[n, lane(core, way, r)] = key_rows(n, way, r, core, own_near[r][own_index[n], way], got)
                    x[n, lane(1 - core, way, r)] = key_rows(n, way, r, 1 - core, own_far[r, own_index[n], way], got)

    scale = 1.0 / math.sqrt(HD)
    pairs = [(c, h, slice(64 * c, 64 * c + 64), slice(128 * h, 128 * h + 128)) for c in range(4) for h in range(2)]
    scores = [lax.dot_general(q[t, e], k[c, :, e], NT, preferred_element_type=f32) * scale for c, h, t, e in pairs]
    for (c, h, t, e), s in zip(pairs, scores):
        p = jnp.exp(s - jnp.max(s, axis=-1, keepdims=True))
        probs[c, h] = p / jnp.sum(p, axis=-1, keepdims=True)
    for c, h, t, e in pairs:
        small[0, t, e] = jnp.dot(probs[c, h].astype(bf), v[c, :, e], preferred_element_type=f32).astype(bf)
    small[2] = small[0].astype(f32).T.astype(bf)

    def backward():
        dprobs = [lax.dot_general(dm[t, e], v[c, :, e], NT, preferred_element_type=f32) for c, h, t, e in pairs]
        for i, (c, h, t, e) in enumerate(pairs):
            p, dprob = probs[c, h], dprobs[i]
            dscore[i] = (p * (dprob - jnp.sum(dprob * p, axis=-1, keepdims=True)) * scale).astype(bf)
        for i, (c, h, t, e) in enumerate(pairs):
            small[1, t, e] = jnp.dot(dscore[i], k[c, :, e], preferred_element_type=f32).astype(bf)
        small[3] = small[1].astype(f32).T.astype(bf)

    def backward_rows():
        for i, (c, h, t, e) in enumerate(pairs):
            keys = slice(256 * c, 256 * c + 256)
            dvt[e, keys] = lax.dot_general(dm[t, e], probs[c, h].astype(bf), TN, preferred_element_type=f32).astype(bf)
            dkt[e, keys] = lax.dot_general(q[t, e], dscore[i], TN, preferred_element_type=f32).astype(bf)

    def nth(i):
        a = jnp.where(i < 4, i, jnp.where(i < 7, 0, 1 + (i - 7) // 3))
        b = jnp.where(i < 4, 0, jnp.where(i < 7, i - 3, 1 + (i - 7) % 3))
        return lax.rem(px + 2 + a, 4) * 4 + lax.rem(pz + 2 + b, 4)

    def fill_flat(place_of, left, right, lo=0, hi=16):
        def step(i, carry):
            j = nth(i)
            cols = pl.ds(pl.multiple_of(j * 256, 256), 256)
            weights[place_of, j] = jnp.dot(left[...], right[:, cols], preferred_element_type=f32).astype(bf)
            return carry
        lax.fori_loop(lo, hi, step, 0, unroll=hi - lo)

    def fill_rows(place_of, left, lo=0, hi=16):
        def step(i, carry):
            cols = pl.ds(pl.multiple_of(nth(i) * 256, 256), 256)
            value = jnp.dot(left[...], x[:, :, cols].reshape(1024, 256), preferred_element_type=f32).astype(bf)
            got[4 * place_of:4 * place_of + 4, :, :, cols] = value.reshape(4, 4, 16, 256)
            return carry
        lax.fori_loop(lo, hi, step, 0, unroll=hi - lo)

    def fill_out(u, left, w, flip):
        dims = (((1,), (1 if flip else 0,)), ((), ()))

        def step(j, carry):
            e = j // 2
            value = lax.dot_general(left[...], weights[w, j], dims, preferred_element_type=f32)
            cols = pl.ds(pl.multiple_of((j % 2) * 256, 256), 256)
            outs[u, e % 2, e // 2, :, cols] = value.astype(bf)
            return carry
        lax.fori_loop(0, 16, step, 0, unroll=8)

    ranks = (2, -1, 1, 0)

    def sum_tree(w, h):
        t = 2 * w + h
        first, second = h, 1 - h
        flat = w in (0, 3)
        if flat:
            b = 2 * (w == 0) + h
            half1, full1, half2, full2 = half_a.at[b], full_a.at[b], half2_a.at[b], full2_a.at[b]
        else:
            b = 2 * (w == 1) + h
            half1, full1, half2, full2 = half_b.at[b], full_b.at[b], half2_b.at[b], full2_b.at[b]

        def block(o1, o2, part=None):
            j = dp_of(first, o1, o2)
            if flat:
                if part is None:
                    return weights.at[int(w == 0), j, pl.ds(128 * h, 128)]
                return weights.at[int(w == 0), j, pl.ds(128 * h + 64 * part, 64)]
            cols = pl.ds(pl.multiple_of(j * 256, 256), 256)
            if part is None:
                return got.at[pl.ds(2 * b, 2), :, :, cols]
            return got.at[2 * b + part, :, :, cols]

        def push(group, src, dst, axis, by):
            remote(src, dst, sum_send.at[t], sum_recv.at[t, group], {"dp": dp_at(axis, by)}).start()

        def landed(group, ref):
            remote(ref, ref, sum_send.at[t], sum_recv.at[t, group], {"dp": dp_at(0, 1)}).wait_recv()

        def s1(i):
            def event():
                push(i, block(ranks[i], 2, 0), half1.at[i, 0], second, 1)
                push(i, block(ranks[i], 2, 1), half1.at[i, 1], second, -1)
            return event

        def s2(i):
            def event():
                landed(i, half1.at[i])
                add_to(block(ranks[i], 1, 0), half1.at[i, 0])
                push(4 + i, block(ranks[i], 1), full1.at[i, 0], second, 1)
                add_to(block(ranks[i], -1, 1), half1.at[i, 1])
                push(4 + i, block(ranks[i], -1), full1.at[i, 1], second, -1)
            return event

        def s3(i):
            def event():
                landed(4 + i, full1.at[i])
                add_to(block(ranks[i], 0), full1.at[i, 0], full1.at[i, 1])
            return event

        def s4():
            push(8, block(2, 0, 0), half2.at[0], first, 1)
            push(8, block(2, 0, 1), half2.at[1], first, -1)

        def s5():
            landed(8, half2)
            add_to(block(1, 0, 0), half2.at[0])
            push(9, block(1, 0), full2.at[0], first, 1)
            add_to(block(-1, 0, 1), half2.at[1])
            push(9, block(-1, 0), full2.at[1], first, -1)

        def s6():
            landed(9, full2)
            value = block(0, 0)[...].astype(f32) + full2[0].astype(f32) + full2[1].astype(f32)
            square[w, pl.ds(128 * h, 128), :] = value.astype(bf).reshape(128, 256)

        return [s1(0), s1(1), s1(2), s1(3)], [
            s2(0), s2(1), s2(2), s2(3), s3(0), s4, s3(1), s3(2), s5, s3(3), s6]

    def output(u, final):
        def push(group, src, dst, target):
            remote(src, dst, out_send.at[u, group], out_recv.at[u, group], target).start()

        def landed(group, ref):
            remote(ref, ref, out_send.at[u, group], out_recv.at[u, group], sibling).wait_recv()

        ahead, behind = {"enc": enc_at(1)}, {"enc": enc_at(-1)}
        top, bottom = pl.ds(0, 128), pl.ds(128, 128)

        def block(by, part=None):
            if part is None:
                return outs.at[u, core, around(y, by)]
            return outs.at[u, core, around(y, by), (top, bottom)[part]]

        def p0():
            push(0, outs.at[u, 1 - core], pair_got.at[u], sibling)

        def p1():
            landed(0, pair_got.at[u])
            add_to(block(2), pair_got.at[u, around(y, 2)])
            push(1, block(2, 0), ring_half.at[u, 0], ahead)
            push(1, block(2, 1), ring_half.at[u, 1], behind)
            for by in (1, -1, 0):
                add_to(block(by), pair_got.at[u, around(y, by)])

        def p2():
            landed(1, ring_half.at[u])
            add_to(block(1, 0), ring_half.at[u, 0])
            push(2, block(1), ring_full.at[u, 0], ahead)
            add_to(block(-1, 1), ring_half.at[u, 1])
            push(2, block(-1), ring_full.at[u, 1], behind)

        def p3():
            landed(2, ring_full.at[u])
            value = (block(0)[...].astype(jnp.float32) + ring_full[u, 0].astype(jnp.float32)
                     + ring_full[u, 1].astype(jnp.float32))
            final[...] = value.astype(jnp.bfloat16)

        return [p0, p1, p2, p3]

    outs0, outs1 = output(0, wide.at[0]), output(1, wide.at[1])
    lists = {w: (sum_tree(w, 0), sum_tree(w, 1)) for w in (3, 2, 1, 0)}

    def begin(w):
        for k in range(4):
            lists[w][0][0][k]()
            lists[w][1][0][k]()

    def then(w, lo, hi):
        for k in range(lo, hi):
            lists[w][0][1][k]()
            lists[w][1][1][k]()

    for w in range(4):
        tree_sent(w)
    for u in range(UNITS - STAGES, UNITS):
        staged_sent(u)
    remote(got.at[:, pl.ds(0, 2)], got.at[:, pl.ds(0, 2)], pair_send, pair_recv.at[0], sibling).wait_send()
    for copy in swaps + backs:
        copy.wait_send()
    fill_flat(0, small.at[2], cot, 0, 7)
    begin(3)
    fill_flat(0, small.at[2], cot, 7, 16)
    fill_out(0, small.at[0], 3, False)
    outs0[0]()
    backward()
    fill_flat(1, small.at[3], tok, 0, 7)
    begin(0)
    then(3, 0, 2)
    fill_flat(1, small.at[3], tok, 7, 16)
    then(3, 2, 4)
    backward_rows()
    order_rows()
    fill_rows(0, dvt, 0, 7)
    begin(2)
    then(0, 0, 2)
    fill_rows(0, dvt, 7, 16)
    then(0, 2, 4)
    fill_rows(1, dkt, 0, 7)
    begin(1)
    then(2, 0, 2)
    outs0[1]()
    fill_rows(1, dkt, 7, 16)
    then(2, 2, 4)
    then(3, 4, 8)
    fill_out(1, small.at[1], 2, True)
    outs1[0]()
    outs0[2]()
    then(0, 4, 8)
    then(1, 0, 4)
    outs1[1]()
    then(3, 8, 10)
    outs0[3]()
    then(2, 4, 8)
    outs1[2]()
    then(0, 8, 10)
    then(1, 4, 8)
    then(3, 10, 11)
    then(2, 8, 10)
    outs1[3]()
    then(0, 10, 11)
    then(1, 8, 10)
    then(2, 10, 11)
    then(1, 10, 11)
    for t in range(TREES):
        ref = weights.at[3, pl.ds(0, 15), pl.ds(0, 128)]
        remote(ref, ref, sum_send.at[t], sum_recv.at[t, 0], sibling).wait_send()
    for u in (0, 1):
        for group, ref in enumerate((pair_got.at[u], ring_half.at[u], ring_full.at[u])):
            remote(ref, ref, out_send.at[u, group], out_recv.at[u, group], sibling).wait_send()


def layer(holder, rows, store, wk, wv, wq, wo, tokens, cotangent):
    bf = jnp.bfloat16
    dma = pltpu.SemaphoreType.DMA
    vm = pltpu.VMEM
    return pl.pallas_call(
        layer_kernel,
        out_shape=(jax.ShapeDtypeStruct((2, 256, 512), bf), jax.ShapeDtypeStruct((4, 256, 256), bf)),
        in_specs=[SMEM, SMEM] + [ANY] * 7,
        out_specs=(VMEM, VMEM),
        scratch_shapes=[
            vm((8, 128, 4096), bf),
            vm((2 * CAP, 2, 16, 4096), bf),
            vm((2 * CAP, 2, 16, 4096), bf),
            vm((2, 2 * CAP, 2, 16, 4096), bf),
            vm((UNITS, 4, 16, 4096), bf),
            vm((STAGES, 2, 16, 4096), bf),
            vm((4, 16, 256, 256), bf),
            vm((256, 4096), bf),
            vm((256, 4096), bf),
            vm((2, 2 * CAP, 2, 16, 256), bf),
            vm((2, 2 * CAP, 2, 16, 256), bf),
            vm((UNITS, 4, 16, 256), bf),
            vm((2, 2 * CAP, 2, 16, 256), bf),
            vm((2, 2 * CAP, 2, 16, 256), bf),
            vm((UNITS, 4, 16, 256), bf),
            vm((256, 256), bf),
            vm((4, 256, 256), bf),
            vm((4, 256, 256), bf),
            vm((256, 256), bf),
            vm((4, 2, 64, 256), jnp.float32),
            vm((8, 64, 256), bf),
            vm((4, 256, 256), bf),
            vm((256, 1024), bf),
            vm((256, 1024), bf),
            vm((2, 2, 4, 256, 512), bf),
            vm((4, 4, 2, 64, 256), bf),
            vm((4, 4, 2, 128, 256), bf),
            vm((4, 4, 2, 4, 16, 256), bf),
            vm((4, 4, 2, 2, 4, 16, 256), bf),
            vm((4, 2, 64, 256), bf),
            vm((4, 2, 128, 256), bf),
            vm((4, 2, 4, 16, 256), bf),
            vm((4, 2, 2, 4, 16, 256), bf),
            vm((2, 4, 256, 512), bf),
            vm((2, 2, 128, 512), bf),
            vm((2, 2, 256, 512), bf),
            dma((7,)),
            dma((4,)),
            dma((4, TREE_SEMS)),
            dma((STAGES,)),
            dma((UNITS,)),
            dma(()),
            dma((5,)),
            dma((4,)),
            dma((4,)),
            dma((TREES,)),
            dma((TREES, SUM_SEMS)),
            dma((2, 3)),
            dma((2, 3)),
        ],
        compiler_params=pltpu.CompilerParams(
            collective_id=0, has_side_effects=True, vmem_limit_bytes=62 * 1024 * 1024),
        name="layer",
    )(holder, rows, store, wk, wv, wq, wo, tokens, cotangent)


def finish_kernel(wide, square, cca, gtok, gq, gk, gv, go_out):
    cca[...] = wide[0]
    gtok[...] = wide[1]
    for w, out in ((0, gq), (1, gk), (2, gv)):
        out[...] = square[w].astype(jnp.float32).T.astype(jnp.bfloat16)
    go_out[...] = square[3]


def finish(wide, square):
    bf = jnp.bfloat16
    return pl.pallas_call(
        finish_kernel,
        out_shape=(jax.ShapeDtypeStruct((256, 512), bf),) * 2 + (jax.ShapeDtypeStruct((256, 256), bf),) * 4,
        in_specs=[VMEM] * 2,
        out_specs=(VMEM,) * 6,
        name="finish",
    )(wide, square)


def body(tokens, store, holder, rows, wq, wk, wv, wo, cotangent):
    return finish(*layer(holder.reshape(8), rows, store, wk, wv, wq, wo, tokens, cotangent))


def solution(mesh):
    placed = (
        P("dp", None), P(("dp", "enc"), None, None), P("dp", None), P("dp"),
        P("dp", "enc"), P("dp", "enc"), P("dp", "enc"), P("enc", "dp"), P("dp", None),
    )
    return jax.shard_map(
        body, mesh=mesh, in_specs=placed,
        out_specs=(P("dp", "enc"),) * 5 + (P("enc", "dp"),),
        check_vma=False,
    )
```

```python
import functools
import math

import jax
import jax.numpy as jnp
from jax import lax
from jax.experimental import pallas as pl
from jax.experimental.pallas import tpu as pltpu
from jax.sharding import PartitionSpec as P

ANY = pl.BlockSpec(memory_space=pl.ANY)
VMEM = pl.BlockSpec(memory_space=pltpu.VMEM)
SMEM = pl.BlockSpec(memory_space=pltpu.SMEM)
HD = 128
CAP = 3
UNITS = 18
STAGES = 6
TREE_SPAN = 18
UNROLL = 1
TREES = 8
SUM_SEMS = 10
TREE_SEMS = 7
NT = (((1,), (1,)), ((), ()))
TN = (((0,), (0,)), ((), ()))


def place():
    dp = lax.axis_index("dp")
    enc = lax.axis_index("enc")
    return dp // 4, dp % 4, enc // 2, enc % 2


def around(value, by):
    return lax.rem(value + (4 + by), 4)


def remote(src, dst, send, recv, target):
    return pltpu.make_async_remote_copy(
        src_ref=src, dst_ref=dst, send_sem=send, recv_sem=recv,
        device_id=target, device_id_type=pl.DeviceIdType.MESH,
    )


def count_if(flag):
    return jnp.where(flag, 1, 0)


def routes(holder, rows, y, core):
    owner = [holder[n] for n in range(8)]
    row = [rows[n] for n in range(8)]
    chip = [o // 2 for o in owner]
    here = [c == y for c in chip]
    rank, chip_rank = [], []
    for n in range(8):
        a, b = jnp.int32(0), jnp.int32(0)
        for m in range(n):
            a += count_if(owner[m] == owner[n])
            b += count_if(chip[m] == chip[n])
        rank.append(a)
        chip_rank.append(b)
    picks = []
    for k in range(CAP):
        value = jnp.int32(0)
        for n in range(8):
            value += jnp.where(jnp.logical_and(owner[n] == y * 2 + core, rank[n] == k), row[n], 0)
        picks.append(value)
    capped = [jnp.minimum(r, CAP - 1) for r in rank]
    own_index = [jnp.where(owner[n] % 2 == core, capped[n], CAP + capped[n]) for n in range(8)]
    order = []
    for t in range(2 * CAP):
        value = jnp.int32(0)
        for n in range(8):
            value += jnp.where(jnp.logical_and(here[n], chip_rank[n] == t), own_index[n], 0)
        order.append(value)

    def held(c):
        value = jnp.int32(0)
        for n in range(8):
            value += count_if(chip[n] == c)
        return value

    n_here = held(y)
    spots = []
    for sign in (1, -1):
        near = 2 * jnp.maximum(held(around(y, -sign)), 1)
        mid = 2 * jnp.maximum(held(around(y, -2 * sign)), 1)
        spot = []
        for n in range(8):
            hops = lax.rem((y - chip[n]) * sign + 4, 4)
            at = 2 * chip_rank[n] + jnp.where(hops > 1, near, 0) + jnp.where(hops > 2, mid, 0)
            spot.append(jnp.minimum(at, UNITS - 2))
        spots.append(spot)
    return picks, order, n_here, here, own_index, spots


def add_to(dst, *parts):
    value = dst[...].astype(jnp.float32)
    for part in parts:
        value += part[...].astype(jnp.float32)
    dst[...] = value.astype(jnp.bfloat16)


def layer_kernel(holder, rows_in, store, wk, wv, wq, wo, tok_in, cot_in,
                 wide, square,
                 x, own_first, own_second, own_far, got, staged, weights, tok, cot,
                 kown_near, kown_far, kgot, vown_near, vown_far, vgot, q, k, v, dm, probs, dscore, small, dkt, dvt,
                 outs, half_a, full_a, half_b, full_b, half2_a, full2_a, half2_b, full2_b,
                 pair_got, ring_half, ring_full,
                 load_sem, tree_send, tree_recv, ring_send, ring_recv, pair_send, pair_recv,
                 own_send, own_recv, sum_send, sum_recv, out_send, out_recv):
    f32, bf = jnp.float32, jnp.bfloat16
    px, pz, y, core = place()
    dp = px * 4 + pz
    sources = (wk, wv, wq, wo)
    own_near = (own_first, own_second)

    def dp_at(axis, by):
        if axis == 0:
            return around(px, by) * 4 + pz
        return px * 4 + around(pz, by)

    def dp_of(first, o1, o2):
        if first == 0:
            return around(px, o1) * 4 + around(pz, o2)
        return around(px, o2) * 4 + around(pz, o1)

    def enc_at(by):
        return around(y, by) * 2 + core

    sibling = {"enc": y * 2 + 1 - core}
    load_store = pltpu.make_async_copy(store, x, load_sem.at[0])
    load_store.start()
    keeps = []
    for i in range(4):
        copy = pltpu.make_async_copy(sources[i], weights.at[i, dp], load_sem.at[1 + i])
        copy.start()
        keeps.append(copy)
    load_tok = pltpu.make_async_copy(tok_in, tok, load_sem.at[5])
    load_cot = pltpu.make_async_copy(cot_in, cot, load_sem.at[6])

    barrier = pltpu.get_barrier_semaphore()
    peers = ([{"dp": dp_at(a, b)} for a in (0, 1) for b in (1, -1)]
             + [{"enc": enc_at(1)}, {"enc": enc_at(-1)}, sibling])
    for peer in peers:
        pl.semaphore_signal(barrier, inc=1, device_id=peer, device_id_type=pl.DeviceIdType.MESH)
    picks, order, n_here, here, own_index, spots = routes(holder, rows_in, y, core)
    lag = 2 * jnp.maximum(n_here, 1)
    load_store.wait()

    def lane(of, way, r):
        return pl.ds(of * 64 + way * 32 + r * 16, 16)

    for r in (0, 1):
        for i in range(CAP):
            for way in (0, 1):
                own_far[r, i, way] = x[picks[i], lane(1 - core, way, r)]
                own_near[r][i, way] = x[picks[i], lane(core, way, r)]
    pl.semaphore_wait(barrier, len(peers))

    def slot(w, j, part=None):
        if part is None:
            return weights.at[w, j]
        return weights.at[w, j, pl.ds(part * 128, 128)]

    def push(w, group, src, dst, axis, by):
        remote(src, dst, tree_send.at[w], tree_recv.at[w, group], {"dp": dp_at(axis, by)}).start()

    def landed(w, group, pieces):
        ref = weights.at[w, pl.ds(0, pieces)]
        remote(ref, ref, tree_send.at[w], tree_recv.at[w, group], {"dp": dp_at(0, 1)}).wait_recv()

    def tree_sent(w):
        ref = weights.at[w, pl.ds(0, 15)]
        remote(ref, ref, tree_send.at[w], tree_recv.at[w, 0], {"dp": dp_at(0, 1)}).wait_send()

    offsets = (0, -1, 1, 2)

    def tree_events(w):
        first = w % 2
        second = 1 - first
        own_block = sources[w]

        def spread(i, src, j):
            push(w, 2 + i, src, slot(w, j), second, 1)
            push(w, 2 + i, src, slot(w, j), second, -1)

        def e0():
            push(w, 0, own_block, slot(w, dp), first, 1)
            push(w, 0, own_block, slot(w, dp), first, -1)

        def e1():
            spread(0, own_block, dp)

        def e2():
            landed(w, 0, 2)
            behind, ahead = dp_of(first, -1, 0), dp_of(first, 1, 0)
            push(w, 1, slot(w, behind, 0), slot(w, behind, 0), first, 1)
            push(w, 1, slot(w, ahead, 1), slot(w, ahead, 1), first, -1)
            spread(1, slot(w, behind), behind)
            spread(2, slot(w, ahead), ahead)

        def e3():
            landed(w, 1, 1)
            j = dp_of(first, 2, 0)
            spread(3, slot(w, j), j)

        def forward(i):
            def event():
                landed(w, 2 + i, 2)
                j = dp_of(first, offsets[i], -1)
                push(w, 6, slot(w, j, 0), slot(w, j, 0), second, 1)
                j = dp_of(first, offsets[i], 1)
                push(w, 6, slot(w, j, 1), slot(w, j, 1), second, -1)
            return event

        def last():
            landed(w, 6, 4)

        return [e0, e1, e2, forward(0), e3, forward(1), forward(2), forward(3), last]

    per = [tree_events(w) for w in range(4)]
    queue = []
    ends = {}
    for pair in ((0, 1), (2, 3)):
        for i in range(9):
            for w in pair:
                queue.append((i + 6 * (w // 2), w, i))
    queue.sort()
    for w in range(4):
        ends[w] = queue.index((8 + 6 * (w // 2), w, 8)) + 1
    queue = [per[w][i] for _, w, i in queue]
    total = len(queue)
    done = [0]

    def advance(upto):
        while done[0] < min(upto, total):
            queue[done[0]]()
            done[0] += 1

    swaps = [remote(own_far.at[r, pl.ds(0, CAP)], own_near[r].at[pl.ds(CAP, CAP)], own_send.at[r], own_recv.at[r], sibling)
             for r in (0, 1)]
    backs = [remote(own_near[r].at[pl.ds(0, CAP)], own_far.at[r, pl.ds(CAP, CAP)], own_send.at[2 + r], own_recv.at[2 + r], sibling)
             for r in (0, 1)]
    swaps[0].start()
    advance(2)
    swaps[1].start()
    load_tok.start()
    load_cot.start()
    advance(4)

    groups = ((0, 4), (4, 8), (8, 12), (12, 16), (16, 18))
    group_of = [i for i, (lo, hi) in enumerate(groups) for _ in range(lo, hi)]

    def pair_wait(group):
        lo, hi = groups[group]
        ref = got.at[pl.ds(lo, hi - lo), pl.ds(2 * (1 - core), 2)]
        remote(ref, ref, pair_send, pair_recv.at[group], sibling).wait_recv()

    def project(w, value):
        return jnp.dot(value, weights[w].reshape(4096, 256), preferred_element_type=f32).astype(bf)

    def kv_near():
        advance(ends[1])
        for copy in keeps[:2]:
            copy.wait()
        for r in (0, 1):
            value = own_near[r][...].reshape(192, 4096)
            kown_near[r] = project(0, value).reshape(6, 2, 16, 256)
            vown_near[r] = project(1, value).reshape(6, 2, 16, 256)

    def kv_far():
        for copy in backs:
            copy.wait_recv()
        value = own_far[...].reshape(384, 4096)
        kown_far[...] = project(0, value).reshape(2, 6, 2, 16, 256)
        vown_far[...] = project(1, value).reshape(2, 6, 2, 16, 256)

    def kv_got(group):
        def event():
            lo, hi = groups[group]
            pair_wait(group)
            value = got[lo:hi].reshape((hi - lo) * 64, 4096)
            kgot[lo:hi] = project(0, value).reshape(hi - lo, 4, 16, 256)
            vgot[lo:hi] = project(1, value).reshape(hi - lo, 4, 16, 256)
        return event

    def queries():
        advance(ends[2])
        keeps[2].wait()
        load_tok.wait()
        q[...] = project(2, tok[...])

    def upstream():
        advance(ends[3])
        keeps[3].wait()
        load_cot.wait()
        acc = jnp.zeros((256, 256), f32)
        for j in range(16):
            acc += lax.dot_general(cot[:, 256 * j:256 * j + 256], weights[3, j], NT, preferred_element_type=f32)
        dm[...] = acc.astype(bf)

    def ring_ref(u):
        return got.at[u, pl.ds(2 * core, 2)]

    def staged_sent(u):
        ref = staged.at[u % STAGES]
        remote(ref, ref, ring_send.at[u % STAGES], ring_recv.at[u], sibling).wait_send()

    work = {11: kv_near, 12: kv_far, 13: kv_got(0), 14: kv_got(1), 15: queries, 16: kv_got(2),
            18: upstream, 19: kv_got(3)}
    for u in range(UNITS + 2):
        if u >= 2:
            remote(ring_ref(u - 2), ring_ref(u - 2), ring_send.at[0], ring_recv.at[u - 2], sibling).wait_recv()
        if u < UNITS:
            if u < 2:
                swaps[u].wait_recv()
            if u >= STAGES:
                staged_sent(u - STAGES)
            for way in (0, 1):
                value = own_near[u % 2][order[min(u // 2, 5)], way]
                for back in (2, 4, 6, 8, 10, 12):
                    if u - back >= 0:
                        use = jnp.logical_and(2 * n_here <= u, lag == back)
                        value = jnp.where(use, got[u - back, 2 * core + way], value)
                staged[u % STAGES, way] = value
                remote(staged.at[u % STAGES, way], got.at[u, 2 * core + way],
                       ring_send.at[u % STAGES], ring_recv.at[u], {"enc": enc_at(1 - 2 * way)}).start()
        if u >= 2:
            remote(ring_ref(u - 2), ring_ref(u - 2), pair_send, pair_recv.at[group_of[u - 2]], sibling).start()
        if u in (2, 3):
            backs[u - 2].start()
        advance(4 + (total - 4) * u // TREE_SPAN)
        if u in work:
            work[u]()
    advance(total)
    kv_got(4)()

    def key_rows(n, way, r, of, own, pool):
        return jnp.where(here[n], own, pool[spots[way][n] + r, 2 * of + way])

    for n in range(8):
        for way in (0, 1):
            for r in (0, 1):
                at = pl.ds((n % 2) * 128 + core * 64 + way * 32 + r * 16, 16)
                k[n // 2, at] = key_rows(n, way, r, core, kown_near[r, own_index[n], way], kgot)
                v[n // 2, at] = key_rows(n, way, r, core, vown_near[r, own_index[n], way], vgot)
                at = pl.ds((n % 2) * 128 + (1 - core) * 64 + way * 32 + r * 16, 16)
                k[n // 2, at] = key_rows(n, way, r, 1 - core, kown_far[r, own_index[n], way], kgot)
                v[n // 2, at] = key_rows(n, way, r, 1 - core, vown_far[r, own_index[n], way], vgot)

    def order_rows():
        for n in range(8):
            for way in (0, 1):
                for r in (0, 1):
                    x[n, lane(core, way, r)] = key_rows(n, way, r, core, own_near[r][own_index[n], way], got)
                    x[n, lane(1 - core, way, r)] = key_rows(n, way, r, 1 - core, own_far[r, own_index[n], way], got)

    scale = 1.0 / math.sqrt(HD)
    pairs = [(c, h, slice(64 * c, 64 * c + 64), slice(128 * h, 128 * h + 128)) for c in range(4) for h in range(2)]
    scores = [lax.dot_general(q[t, e], k[c, :, e], NT, preferred_element_type=f32) * scale for c, h, t, e in pairs]
    for (c, h, t, e), s in zip(pairs, scores):
        p = jnp.exp(s - jnp.max(s, axis=-1, keepdims=True))
        probs[c, h] = p / jnp.sum(p, axis=-1, keepdims=True)
    for c, h, t, e in pairs:
        small[0, t, e] = jnp.dot(probs[c, h].astype(bf), v[c, :, e], preferred_element_type=f32).astype(bf)
    small[2] = small[0].astype(f32).T.astype(bf)

    def backward():
        dprobs = [lax.dot_general(dm[t, e], v[c, :, e], NT, preferred_element_type=f32) for c, h, t, e in pairs]
        for i, (c, h, t, e) in enumerate(pairs):
            p, dprob = probs[c, h], dprobs[i]
            dscore[i] = (p * (dprob - jnp.sum(dprob * p, axis=-1, keepdims=True)) * scale).astype(bf)
        for i, (c, h, t, e) in enumerate(pairs):
            small[1, t, e] = jnp.dot(dscore[i], k[c, :, e], preferred_element_type=f32).astype(bf)
        small[3] = small[1].astype(f32).T.astype(bf)

    def backward_rows():
        for i, (c, h, t, e) in enumerate(pairs):
            keys = slice(256 * c, 256 * c + 256)
            dvt[e, keys] = lax.dot_general(dm[t, e], probs[c, h].astype(bf), TN, preferred_element_type=f32).astype(bf)
            dkt[e, keys] = lax.dot_general(q[t, e], dscore[i], TN, preferred_element_type=f32).astype(bf)

    def nth(i):
        a = jnp.where(i < 4, i, jnp.where(i < 7, 0, 1 + (i - 7) // 3))
        b = jnp.where(i < 4, 0, jnp.where(i < 7, i - 3, 1 + (i - 7) % 3))
        return lax.rem(px + 2 + a, 4) * 4 + lax.rem(pz + 2 + b, 4)

    def fill_flat(place_of, left, right, lo=0, hi=16):
        def step(i, carry):
            j = nth(i)
            cols = pl.ds(pl.multiple_of(j * 256, 256), 256)
            weights[place_of, j] = jnp.dot(left[...], right[:, cols], preferred_element_type=f32).astype(bf)
            return carry
        lax.fori_loop(lo, hi, step, 0, unroll=hi - lo)

    def fill_rows(place_of, left, lo=0, hi=16):
        def step(i, carry):
            cols = pl.ds(pl.multiple_of(nth(i) * 256, 256), 256)
            value = jnp.dot(left[...], x[:, :, cols].reshape(1024, 256), preferred_element_type=f32).astype(bf)
            got[4 * place_of:4 * place_of + 4, :, :, cols] = value.reshape(4, 4, 16, 256)
            return carry
        lax.fori_loop(lo, hi, step, 0, unroll=hi - lo)

    def fill_out(u, left, w, flip):
        dims = (((1,), (1 if flip else 0,)), ((), ()))

        def step(j, carry):
            e = j // 2
            value = lax.dot_general(left[...], weights[w, j], dims, preferred_element_type=f32)
            cols = pl.ds(pl.multiple_of((j % 2) * 256, 256), 256)
            outs[u, e % 2, e // 2, :, cols] = value.astype(bf)
            return carry
        lax.fori_loop(0, 16, step, 0, unroll=8)

    ranks = (2, -1, 1, 0)

    def sum_tree(w, h):
        t = 2 * w + h
        first, second = h, 1 - h
        flat = w in (0, 3)
        if flat:
            b = 2 * (w == 0) + h
            half1, full1, half2, full2 = half_a.at[b], full_a.at[b], half2_a.at[b], full2_a.at[b]
        else:
            b = 2 * (w == 1) + h
            half1, full1, half2, full2 = half_b.at[b], full_b.at[b], half2_b.at[b], full2_b.at[b]

        def block(o1, o2, part=None):
            j = dp_of(first, o1, o2)
            if flat:
                if part is None:
                    return weights.at[int(w == 0), j, pl.ds(128 * h, 128)]
                return weights.at[int(w == 0), j, pl.ds(128 * h + 64 * part, 64)]
            cols = pl.ds(pl.multiple_of(j * 256, 256), 256)
            if part is None:
                return got.at[pl.ds(2 * b, 2), :, :, cols]
            return got.at[2 * b + part, :, :, cols]

        def push(group, src, dst, axis, by):
            remote(src, dst, sum_send.at[t], sum_recv.at[t, group], {"dp": dp_at(axis, by)}).start()

        def landed(group, ref):
            remote(ref, ref, sum_send.at[t], sum_recv.at[t, group], {"dp": dp_at(0, 1)}).wait_recv()

        def s1(i):
            def event():
                push(i, block(ranks[i], 2, 0), half1.at[i, 0], second, 1)
                push(i, block(ranks[i], 2, 1), half1.at[i, 1], second, -1)
            return event

        def s2(i):
            def event():
                landed(i, half1.at[i])
                add_to(block(ranks[i], 1, 0), half1.at[i, 0])
                push(4 + i, block(ranks[i], 1), full1.at[i, 0], second, 1)
                add_to(block(ranks[i], -1, 1), half1.at[i, 1])
                push(4 + i, block(ranks[i], -1), full1.at[i, 1], second, -1)
            return event

        def s3(i):
            def event():
                landed(4 + i, full1.at[i])
                add_to(block(ranks[i], 0), full1.at[i, 0], full1.at[i, 1])
            return event

        def s4():
            push(8, block(2, 0, 0), half2.at[0], first, 1)
            push(8, block(2, 0, 1), half2.at[1], first, -1)

        def s5():
            landed(8, half2)
            add_to(block(1, 0, 0), half2.at[0])
            push(9, block(1, 0), full2.at[0], first, 1)
            add_to(block(-1, 0, 1), half2.at[1])
            push(9, block(-1, 0), full2.at[1], first, -1)

        def s6():
            landed(9, full2)
            value = block(0, 0)[...].astype(f32) + full2[0].astype(f32) + full2[1].astype(f32)
            square[w, pl.ds(128 * h, 128), :] = value.astype(bf).reshape(128, 256)

        return [s1(0), s1(1), s1(2), s1(3)], [
            s2(0), s2(1), s2(2), s2(3), s3(0), s4, s3(1), s3(2), s5, s3(3), s6]

    def output(u, final):
        def push(group, src, dst, target):
            remote(src, dst, out_send.at[u, group], out_recv.at[u, group], target).start()

        def landed(group, ref):
            remote(ref, ref, out_send.at[u, group], out_recv.at[u, group], sibling).wait_recv()

        ahead, behind = {"enc": enc_at(1)}, {"enc": enc_at(-1)}
        top, bottom = pl.ds(0, 128), pl.ds(128, 128)

        def block(by, part=None):
            if part is None:
                return outs.at[u, core, around(y, by)]
            return outs.at[u, core, around(y, by), (top, bottom)[part]]

        def p0():
            push(0, outs.at[u, 1 - core], pair_got.at[u], sibling)

        def p1():
            landed(0, pair_got.at[u])
            add_to(block(2), pair_got.at[u, around(y, 2)])
            push(1, block(2, 0), ring_half.at[u, 0], ahead)
            push(1, block(2, 1), ring_half.at[u, 1], behind)
            for by in (1, -1, 0):
                add_to(block(by), pair_got.at[u, around(y, by)])

        def p2():
            landed(1, ring_half.at[u])
            add_to(block(1, 0), ring_half.at[u, 0])
            push(2, block(1), ring_full.at[u, 0], ahead)
            add_to(block(-1, 1), ring_half.at[u, 1])
            push(2, block(-1), ring_full.at[u, 1], behind)

        def p3():
            landed(2, ring_full.at[u])
            value = (block(0)[...].astype(jnp.float32) + ring_full[u, 0].astype(jnp.float32)
                     + ring_full[u, 1].astype(jnp.float32))
            final[...] = value.astype(jnp.bfloat16)

        return [p0, p1, p2, p3]

    outs0, outs1 = output(0, wide.at[0]), output(1, wide.at[1])
    lists = {w: (sum_tree(w, 0), sum_tree(w, 1)) for w in (3, 2, 1, 0)}

    def begin(w):
        for k in range(4):
            lists[w][0][0][k]()
            lists[w][1][0][k]()

    def then(w, lo, hi):
        for k in range(lo, hi):
            lists[w][0][1][k]()
            lists[w][1][1][k]()

    for w in range(4):
        tree_sent(w)
    for u in range(UNITS - STAGES, UNITS):
        staged_sent(u)
    remote(got.at[:, pl.ds(0, 2)], got.at[:, pl.ds(0, 2)], pair_send, pair_recv.at[0], sibling).wait_send()
    for copy in swaps + backs:
        copy.wait_send()
    fill_flat(0, small.at[2], cot, 0, 7)
    begin(3)
    fill_flat(0, small.at[2], cot, 7, 16)
    fill_out(0, small.at[0], 3, False)
    outs0[0]()
    backward()
    fill_flat(1, small.at[3], tok, 0, 7)
    begin(0)
    then(3, 0, 2)
    fill_flat(1, small.at[3], tok, 7, 16)
    then(3, 2, 4)
    backward_rows()
    order_rows()
    fill_rows(0, dvt, 0, 7)
    begin(2)
    then(0, 0, 2)
    fill_rows(0, dvt, 7, 16)
    then(0, 2, 4)
    fill_rows(1, dkt, 0, 7)
    begin(1)
    then(3, 4, 6)
    fill_rows(1, dkt, 7, 16)
    then(2, 0, 2)
    outs0[1]()
    then(2, 2, 4)
    then(3, 6, 8)
    fill_out(1, small.at[1], 2, True)
    outs1[0]()
    outs0[2]()
    then(0, 4, 8)
    then(1, 0, 4)
    outs1[1]()
    then(3, 8, 10)
    outs0[3]()
    then(2, 4, 8)
    outs1[2]()
    then(0, 8, 10)
    then(1, 4, 8)
    then(2, 8, 10)
    then(3, 10, 11)
    then(1, 8, 9)
    then(0, 10, 11)
    then(1, 9, 10)
    outs1[3]()
    then(2, 10, 11)
    then(1, 10, 11)
    for t in range(TREES):
        ref = weights.at[3, pl.ds(0, 15), pl.ds(0, 128)]
        remote(ref, ref, sum_send.at[t], sum_recv.at[t, 0], sibling).wait_send()
    for u in (0, 1):
        for group, ref in enumerate((pair_got.at[u], ring_half.at[u], ring_full.at[u])):
            remote(ref, ref, out_send.at[u, group], out_recv.at[u, group], sibling).wait_send()


def layer(holder, rows, store, wk, wv, wq, wo, tokens, cotangent):
    bf = jnp.bfloat16
    dma = pltpu.SemaphoreType.DMA
    vm = pltpu.VMEM
    return pl.pallas_call(
        layer_kernel,
        out_shape=(jax.ShapeDtypeStruct((2, 256, 512), bf), jax.ShapeDtypeStruct((4, 256, 256), bf)),
        in_specs=[SMEM, SMEM] + [ANY] * 7,
        out_specs=(VMEM, VMEM),
        scratch_shapes=[
            vm((8, 128, 4096), bf),
            vm((2 * CAP, 2, 16, 4096), bf),
            vm((2 * CAP, 2, 16, 4096), bf),
            vm((2, 2 * CAP, 2, 16, 4096), bf),
            vm((UNITS, 4, 16, 4096), bf),
            vm((STAGES, 2, 16, 4096), bf),
            vm((4, 16, 256, 256), bf),
            vm((256, 4096), bf),
            vm((256, 4096), bf),
            vm((2, 2 * CAP, 2, 16, 256), bf),
            vm((2, 2 * CAP, 2, 16, 256), bf),
            vm((UNITS, 4, 16, 256), bf),
            vm((2, 2 * CAP, 2, 16, 256), bf),
            vm((2, 2 * CAP, 2, 16, 256), bf),
            vm((UNITS, 4, 16, 256), bf),
            vm((256, 256), bf),
            vm((4, 256, 256), bf),
            vm((4, 256, 256), bf),
            vm((256, 256), bf),
            vm((4, 2, 64, 256), jnp.float32),
            vm((8, 64, 256), bf),
            vm((4, 256, 256), bf),
            vm((256, 1024), bf),
            vm((256, 1024), bf),
            vm((2, 2, 4, 256, 512), bf),
            vm((4, 4, 2, 64, 256), bf),
            vm((4, 4, 2, 128, 256), bf),
            vm((4, 4, 2, 4, 16, 256), bf),
            vm((4, 4, 2, 2, 4, 16, 256), bf),
            vm((4, 2, 64, 256), bf),
            vm((4, 2, 128, 256), bf),
            vm((4, 2, 4, 16, 256), bf),
            vm((4, 2, 2, 4, 16, 256), bf),
            vm((2, 4, 256, 512), bf),
            vm((2, 2, 128, 512), bf),
            vm((2, 2, 256, 512), bf),
            dma((7,)),
            dma((4,)),
            dma((4, TREE_SEMS)),
            dma((STAGES,)),
            dma((UNITS,)),
            dma(()),
            dma((5,)),
            dma((4,)),
            dma((4,)),
            dma((TREES,)),
            dma((TREES, SUM_SEMS)),
            dma((2, 3)),
            dma((2, 3)),
        ],
        compiler_params=pltpu.CompilerParams(
            collective_id=0, has_side_effects=True, vmem_limit_bytes=62 * 1024 * 1024),
        name="layer",
    )(holder, rows, store, wk, wv, wq, wo, tokens, cotangent)


def finish_kernel(wide, square, cca, gtok, gq, gk, gv, go_out):
    cca[...] = wide[0]
    gtok[...] = wide[1]
    for w, out in ((0, gq), (1, gk), (2, gv)):
        out[...] = square[w].astype(jnp.float32).T.astype(jnp.bfloat16)
    go_out[...] = square[3]


def finish(wide, square):
    bf = jnp.bfloat16
    return pl.pallas_call(
        finish_kernel,
        out_shape=(jax.ShapeDtypeStruct((256, 512), bf),) * 2 + (jax.ShapeDtypeStruct((256, 256), bf),) * 4,
        in_specs=[VMEM] * 2,
        out_specs=(VMEM,) * 6,
        name="finish",
    )(wide, square)


def body(tokens, store, holder, rows, wq, wk, wv, wo, cotangent):
    return finish(*layer(holder.reshape(8), rows, store, wk, wv, wq, wo, tokens, cotangent))


def solution(mesh):
    placed = (
        P("dp", None), P(("dp", "enc"), None, None), P("dp", None), P("dp"),
        P("dp", "enc"), P("dp", "enc"), P("dp", "enc"), P("enc", "dp"), P("dp", None),
    )
    return jax.shard_map(
        body, mesh=mesh, in_specs=placed,
        out_specs=(P("dp", "enc"),) * 5 + (P("enc", "dp"),),
        check_vma=False,
    )
```

```python
import functools
import math

import jax
import jax.numpy as jnp
from jax import lax
from jax.experimental import pallas as pl
from jax.experimental.pallas import tpu as pltpu
from jax.sharding import PartitionSpec as P

ANY = pl.BlockSpec(memory_space=pl.ANY)
VMEM = pl.BlockSpec(memory_space=pltpu.VMEM)
SMEM = pl.BlockSpec(memory_space=pltpu.SMEM)
HD = 128
CAP = 3
UNITS = 18
STAGES = 6
TREE_SPAN = 18
UNROLL = 1
TREES = 8
SUM_SEMS = 10
TREE_SEMS = 7
NT = (((1,), (1,)), ((), ()))
TN = (((0,), (0,)), ((), ()))


def place():
    dp = lax.axis_index("dp")
    enc = lax.axis_index("enc")
    return dp // 4, dp % 4, enc // 2, enc % 2


def around(value, by):
    return lax.rem(value + (4 + by), 4)


def remote(src, dst, send, recv, target):
    return pltpu.make_async_remote_copy(
        src_ref=src, dst_ref=dst, send_sem=send, recv_sem=recv,
        device_id=target, device_id_type=pl.DeviceIdType.MESH,
    )


def count_if(flag):
    return jnp.where(flag, 1, 0)


def routes(holder, rows, y, core):
    owner = [holder[n] for n in range(8)]
    row = [rows[n] for n in range(8)]
    chip = [o // 2 for o in owner]
    here = [c == y for c in chip]
    rank, chip_rank = [], []
    for n in range(8):
        a, b = jnp.int32(0), jnp.int32(0)
        for m in range(n):
            a += count_if(owner[m] == owner[n])
            b += count_if(chip[m] == chip[n])
        rank.append(a)
        chip_rank.append(b)
    picks = []
    for k in range(CAP):
        value = jnp.int32(0)
        for n in range(8):
            value += jnp.where(jnp.logical_and(owner[n] == y * 2 + core, rank[n] == k), row[n], 0)
        picks.append(value)
    capped = [jnp.minimum(r, CAP - 1) for r in rank]
    own_index = [jnp.where(owner[n] % 2 == core, capped[n], CAP + capped[n]) for n in range(8)]
    order = []
    for t in range(2 * CAP):
        value = jnp.int32(0)
        for n in range(8):
            value += jnp.where(jnp.logical_and(here[n], chip_rank[n] == t), own_index[n], 0)
        order.append(value)

    def held(c):
        value = jnp.int32(0)
        for n in range(8):
            value += count_if(chip[n] == c)
        return value

    n_here = held(y)
    spots = []
    for sign in (1, -1):
        near = 2 * jnp.maximum(held(around(y, -sign)), 1)
        mid = 2 * jnp.maximum(held(around(y, -2 * sign)), 1)
        spot = []
        for n in range(8):
            hops = lax.rem((y - chip[n]) * sign + 4, 4)
            at = 2 * chip_rank[n] + jnp.where(hops > 1, near, 0) + jnp.where(hops > 2, mid, 0)
            spot.append(jnp.minimum(at, UNITS - 2))
        spots.append(spot)
    return picks, order, n_here, here, own_index, spots


def add_to(dst, *parts):
    value = dst[...].astype(jnp.float32)
    for part in parts:
        value += part[...].astype(jnp.float32)
    dst[...] = value.astype(jnp.bfloat16)


def layer_kernel(holder, rows_in, store, wk, wv, wq, wo, tok_in, cot_in,
                 wide, square,
                 x, own_first, own_second, own_far, got, staged, weights, tok, cot,
                 kown_near, kown_far, kgot, vown_near, vown_far, vgot, q, k, v, dm, probs, dscore, small, dkt, dvt,
                 outs, half_a, full_a, half_b, full_b, half2_a, full2_a, half2_b, full2_b,
                 pair_got, ring_half, ring_full,
                 load_sem, tree_send, tree_recv, ring_send, ring_recv, pair_send, pair_recv,
                 own_send, own_recv, sum_send, sum_recv, out_send, out_recv):
    f32, bf = jnp.float32, jnp.bfloat16
    px, pz, y, core = place()
    dp = px * 4 + pz
    sources = (wk, wv, wq, wo)
    own_near = (own_first, own_second)

    def dp_at(axis, by):
        if axis == 0:
            return around(px, by) * 4 + pz
        return px * 4 + around(pz, by)

    def dp_of(first, o1, o2):
        if first == 0:
            return around(px, o1) * 4 + around(pz, o2)
        return around(px, o2) * 4 + around(pz, o1)

    def enc_at(by):
        return around(y, by) * 2 + core

    sibling = {"enc": y * 2 + 1 - core}
    load_store = pltpu.make_async_copy(store, x, load_sem.at[0])
    load_store.start()
    keeps = []
    for i in range(4):
        copy = pltpu.make_async_copy(sources[i], weights.at[i, dp], load_sem.at[1 + i])
        copy.start()
        keeps.append(copy)
    load_tok = pltpu.make_async_copy(tok_in, tok, load_sem.at[5])
    load_cot = pltpu.make_async_copy(cot_in, cot, load_sem.at[6])

    barrier = pltpu.get_barrier_semaphore()
    peers = ([{"dp": dp_at(a, b)} for a in (0, 1) for b in (1, -1)]
             + [{"enc": enc_at(1)}, {"enc": enc_at(-1)}, sibling])
    for peer in peers:
        pl.semaphore_signal(barrier, inc=1, device_id=peer, device_id_type=pl.DeviceIdType.MESH)
    picks, order, n_here, here, own_index, spots = routes(holder, rows_in, y, core)
    lag = 2 * jnp.maximum(n_here, 1)
    load_store.wait()

    def lane(of, way, r):
        return pl.ds(of * 64 + way * 32 + r * 16, 16)

    for r in (0, 1):
        for i in range(CAP):
            for way in (0, 1):
                own_far[r, i, way] = x[picks[i], lane(1 - core, way, r)]
                own_near[r][i, way] = x[picks[i], lane(core, way, r)]
    pl.semaphore_wait(barrier, len(peers))

    def slot(w, j, part=None):
        if part is None:
            return weights.at[w, j]
        return weights.at[w, j, pl.ds(part * 128, 128)]

    def push(w, group, src, dst, axis, by):
        remote(src, dst, tree_send.at[w], tree_recv.at[w, group], {"dp": dp_at(axis, by)}).start()

    def landed(w, group, pieces):
        ref = weights.at[w, pl.ds(0, pieces)]
        remote(ref, ref, tree_send.at[w], tree_recv.at[w, group], {"dp": dp_at(0, 1)}).wait_recv()

    def tree_sent(w):
        ref = weights.at[w, pl.ds(0, 15)]
        remote(ref, ref, tree_send.at[w], tree_recv.at[w, 0], {"dp": dp_at(0, 1)}).wait_send()

    offsets = (0, -1, 1, 2)

    def tree_events(w):
        first = w % 2
        second = 1 - first
        own_block = sources[w]

        def spread(i, src, j):
            push(w, 2 + i, src, slot(w, j), second, 1)
            push(w, 2 + i, src, slot(w, j), second, -1)

        def e0():
            push(w, 0, own_block, slot(w, dp), first, 1)
            push(w, 0, own_block, slot(w, dp), first, -1)

        def e1():
            spread(0, own_block, dp)

        def e2():
            landed(w, 0, 2)
            behind, ahead = dp_of(first, -1, 0), dp_of(first, 1, 0)
            push(w, 1, slot(w, behind, 0), slot(w, behind, 0), first, 1)
            push(w, 1, slot(w, ahead, 1), slot(w, ahead, 1), first, -1)
            spread(1, slot(w, behind), behind)
            spread(2, slot(w, ahead), ahead)

        def e3():
            landed(w, 1, 1)
            j = dp_of(first, 2, 0)
            spread(3, slot(w, j), j)

        def forward(i):
            def event():
                landed(w, 2 + i, 2)
                j = dp_of(first, offsets[i], -1)
                push(w, 6, slot(w, j, 0), slot(w, j, 0), second, 1)
                j = dp_of(first, offsets[i], 1)
                push(w, 6, slot(w, j, 1), slot(w, j, 1), second, -1)
            return event

        def last():
            landed(w, 6, 4)

        return [e0, e1, e2, forward(0), e3, forward(1), forward(2), forward(3), last]

    per = [tree_events(w) for w in range(4)]
    queue = []
    ends = {}
    for pair in ((0, 1), (2, 3)):
        for i in range(9):
            for w in pair:
                queue.append((i + 6 * (w // 2), w, i))
    queue.sort()
    for w in range(4):
        ends[w] = queue.index((8 + 6 * (w // 2), w, 8)) + 1
    queue = [per[w][i] for _, w, i in queue]
    total = len(queue)
    done = [0]

    def advance(upto):
        while done[0] < min(upto, total):
            queue[done[0]]()
            done[0] += 1

    swaps = [remote(own_far.at[r, pl.ds(0, CAP)], own_near[r].at[pl.ds(CAP, CAP)], own_send.at[r], own_recv.at[r], sibling)
             for r in (0, 1)]
    backs = [remote(own_near[r].at[pl.ds(0, CAP)], own_far.at[r, pl.ds(CAP, CAP)], own_send.at[2 + r], own_recv.at[2 + r], sibling)
             for r in (0, 1)]
    swaps[0].start()
    advance(2)
    swaps[1].start()
    load_tok.start()
    load_cot.start()
    advance(4)

    groups = ((0, 4), (4, 8), (8, 12), (12, 16), (16, 18))
    group_of = [i for i, (lo, hi) in enumerate(groups) for _ in range(lo, hi)]

    def pair_wait(group):
        lo, hi = groups[group]
        ref = got.at[pl.ds(lo, hi - lo), pl.ds(2 * (1 - core), 2)]
        remote(ref, ref, pair_send, pair_recv.at[group], sibling).wait_recv()

    def project(w, value):
        return jnp.dot(value, weights[w].reshape(4096, 256), preferred_element_type=f32).astype(bf)

    def kv_near():
        advance(ends[1])
        for copy in keeps[:2]:
            copy.wait()
        for r in (0, 1):
            value = own_near[r][...].reshape(192, 4096)
            kown_near[r] = project(0, value).reshape(6, 2, 16, 256)
            vown_near[r] = project(1, value).reshape(6, 2, 16, 256)

    def kv_far():
        for copy in backs:
            copy.wait_recv()
        value = own_far[...].reshape(384, 4096)
        kown_far[...] = project(0, value).reshape(2, 6, 2, 16, 256)
        vown_far[...] = project(1, value).reshape(2, 6, 2, 16, 256)

    def kv_got(group):
        def event():
            lo, hi = groups[group]
            pair_wait(group)
            value = got[lo:hi].reshape((hi - lo) * 64, 4096)
            kgot[lo:hi] = project(0, value).reshape(hi - lo, 4, 16, 256)
            vgot[lo:hi] = project(1, value).reshape(hi - lo, 4, 16, 256)
        return event

    def queries():
        advance(ends[2])
        keeps[2].wait()
        load_tok.wait()
        q[...] = project(2, tok[...])

    def upstream():
        advance(ends[3])
        keeps[3].wait()
        load_cot.wait()
        acc = jnp.zeros((256, 256), f32)
        for j in range(16):
            acc += lax.dot_general(cot[:, 256 * j:256 * j + 256], weights[3, j], NT, preferred_element_type=f32)
        dm[...] = acc.astype(bf)

    def ring_ref(u):
        return got.at[u, pl.ds(2 * core, 2)]

    def staged_sent(u):
        ref = staged.at[u % STAGES]
        remote(ref, ref, ring_send.at[u % STAGES], ring_recv.at[u], sibling).wait_send()

    work = {11: kv_near, 12: kv_far, 13: kv_got(0), 14: kv_got(1), 15: queries, 16: kv_got(2),
            18: upstream, 19: kv_got(3)}
    for u in range(UNITS + 2):
        if u >= 2:
            remote(ring_ref(u - 2), ring_ref(u - 2), ring_send.at[0], ring_recv.at[u - 2], sibling).wait_recv()
        if u < UNITS:
            if u < 2:
                swaps[u].wait_recv()
            if u >= STAGES:
                staged_sent(u - STAGES)
            for way in (0, 1):
                value = own_near[u % 2][order[min(u // 2, 5)], way]
                for back in (2, 4, 6, 8, 10, 12):
                    if u - back >= 0:
                        use = jnp.logical_and(2 * n_here <= u, lag == back)
                        value = jnp.where(use, got[u - back, 2 * core + way], value)
                staged[u % STAGES, way] = value
                remote(staged.at[u % STAGES, way], got.at[u, 2 * core + way],
                       ring_send.at[u % STAGES], ring_recv.at[u], {"enc": enc_at(1 - 2 * way)}).start()
        if u >= 2:
            remote(ring_ref(u - 2), ring_ref(u - 2), pair_send, pair_recv.at[group_of[u - 2]], sibling).start()
        if u in (2, 3):
            backs[u - 2].start()
        advance(4 + (total - 4) * u // TREE_SPAN)
        if u in work:
            work[u]()
    advance(total)
    kv_got(4)()

    def key_rows(n, way, r, of, own, pool):
        return jnp.where(here[n], own, pool[spots[way][n] + r, 2 * of + way])

    for n in range(8):
        for way in (0, 1):
            for r in (0, 1):
                at = pl.ds((n % 2) * 128 + core * 64 + way * 32 + r * 16, 16)
                k[n // 2, at] = key_rows(n, way, r, core, kown_near[r, own_index[n], way], kgot)
                v[n // 2, at] = key_rows(n, way, r, core, vown_near[r, own_index[n], way], vgot)
                at = pl.ds((n % 2) * 128 + (1 - core) * 64 + way * 32 + r * 16, 16)
                k[n // 2, at] = key_rows(n, way, r, 1 - core, kown_far[r, own_index[n], way], kgot)
                v[n // 2, at] = key_rows(n, way, r, 1 - core, vown_far[r, own_index[n], way], vgot)

    def order_rows():
        for n in range(8):
            for way in (0, 1):
                for r in (0, 1):
                    x[n, lane(core, way, r)] = key_rows(n, way, r, core, own_near[r][own_index[n], way], got)
                    x[n, lane(1 - core, way, r)] = key_rows(n, way, r, 1 - core, own_far[r, own_index[n], way], got)

    scale = 1.0 / math.sqrt(HD)
    pairs = [(c, h, slice(64 * c, 64 * c + 64), slice(128 * h, 128 * h + 128)) for c in range(4) for h in range(2)]
    scores = [lax.dot_general(q[t, e], k[c, :, e], NT, preferred_element_type=f32) * scale for c, h, t, e in pairs]
    for (c, h, t, e), s in zip(pairs, scores):
        p = jnp.exp(s - jnp.max(s, axis=-1, keepdims=True))
        probs[c, h] = p * (1.0 / jnp.sum(p, axis=-1, keepdims=True))
    for c, h, t, e in pairs:
        small[0, t, e] = jnp.dot(probs[c, h].astype(bf), v[c, :, e], preferred_element_type=f32).astype(bf)
    small[2] = small[0].astype(f32).T.astype(bf)

    def backward():
        dprobs = [lax.dot_general(dm[t, e], v[c, :, e], NT, preferred_element_type=f32) for c, h, t, e in pairs]
        for i, (c, h, t, e) in enumerate(pairs):
            p, dprob = probs[c, h], dprobs[i]
            dscore[i] = (p * (dprob - jnp.sum(dprob * p, axis=-1, keepdims=True)) * scale).astype(bf)
        for i, (c, h, t, e) in enumerate(pairs):
            small[1, t, e] = jnp.dot(dscore[i], k[c, :, e], preferred_element_type=f32).astype(bf)
        small[3] = small[1].astype(f32).T.astype(bf)

    def backward_rows():
        for i, (c, h, t, e) in enumerate(pairs):
            keys = slice(256 * c, 256 * c + 256)
            dvt[e, keys] = lax.dot_general(dm[t, e], probs[c, h].astype(bf), TN, preferred_element_type=f32).astype(bf)
            dkt[e, keys] = lax.dot_general(q[t, e], dscore[i], TN, preferred_element_type=f32).astype(bf)

    def nth(i):
        a = jnp.where(i < 4, i, jnp.where(i < 7, 0, 1 + (i - 7) // 3))
        b = jnp.where(i < 4, 0, jnp.where(i < 7, i - 3, 1 + (i - 7) % 3))
        return lax.rem(px + 2 + a, 4) * 4 + lax.rem(pz + 2 + b, 4)

    def fill_flat(place_of, left, right, lo=0, hi=16):
        def step(i, carry):
            j = nth(i)
            cols = pl.ds(pl.multiple_of(j * 256, 256), 256)
            weights[place_of, j] = jnp.dot(left[...], right[:, cols], preferred_element_type=f32).astype(bf)
            return carry
        lax.fori_loop(lo, hi, step, 0, unroll=hi - lo)

    def fill_rows(place_of, left, lo=0, hi=16):
        def step(i, carry):
            cols = pl.ds(pl.multiple_of(nth(i) * 256, 256), 256)
            value = jnp.dot(left[...], x[:, :, cols].reshape(1024, 256), preferred_element_type=f32).astype(bf)
            got[4 * place_of:4 * place_of + 4, :, :, cols] = value.reshape(4, 4, 16, 256)
            return carry
        lax.fori_loop(lo, hi, step, 0, unroll=hi - lo)

    def fill_out(u, left, w, flip):
        dims = (((1,), (1 if flip else 0,)), ((), ()))

        def step(j, carry):
            e = j // 2
            value = lax.dot_general(left[...], weights[w, j], dims, preferred_element_type=f32)
            cols = pl.ds(pl.multiple_of((j % 2) * 256, 256), 256)
            outs[u, e % 2, e // 2, :, cols] = value.astype(bf)
            return carry
        lax.fori_loop(0, 16, step, 0, unroll=8)

    ranks = (2, -1, 1, 0)

    def sum_tree(w, h):
        t = 2 * w + h
        first, second = h, 1 - h
        flat = w in (0, 3)
        if flat:
            b = 2 * (w == 0) + h
            half1, full1, half2, full2 = half_a.at[b], full_a.at[b], half2_a.at[b], full2_a.at[b]
        else:
            b = 2 * (w == 1) + h
            half1, full1, half2, full2 = half_b.at[b], full_b.at[b], half2_b.at[b], full2_b.at[b]

        def block(o1, o2, part=None):
            j = dp_of(first, o1, o2)
            if flat:
                if part is None:
                    return weights.at[int(w == 0), j, pl.ds(128 * h, 128)]
                return weights.at[int(w == 0), j, pl.ds(128 * h + 64 * part, 64)]
            cols = pl.ds(pl.multiple_of(j * 256, 256), 256)
            if part is None:
                return got.at[pl.ds(2 * b, 2), :, :, cols]
            return got.at[2 * b + part, :, :, cols]

        def push(group, src, dst, axis, by):
            remote(src, dst, sum_send.at[t], sum_recv.at[t, group], {"dp": dp_at(axis, by)}).start()

        def landed(group, ref):
            remote(ref, ref, sum_send.at[t], sum_recv.at[t, group], {"dp": dp_at(0, 1)}).wait_recv()

        def s1(i):
            def event():
                push(i, block(ranks[i], 2, 0), half1.at[i, 0], second, 1)
                push(i, block(ranks[i], 2, 1), half1.at[i, 1], second, -1)
            return event

        def s2(i):
            def event():
                landed(i, half1.at[i])
                add_to(block(ranks[i], 1, 0), half1.at[i, 0])
                push(4 + i, block(ranks[i], 1), full1.at[i, 0], second, 1)
                add_to(block(ranks[i], -1, 1), half1.at[i, 1])
                push(4 + i, block(ranks[i], -1), full1.at[i, 1], second, -1)
            return event

        def s3(i):
            def event():
                landed(4 + i, full1.at[i])
                add_to(block(ranks[i], 0), full1.at[i, 0], full1.at[i, 1])
            return event

        def s4():
            push(8, block(2, 0, 0), half2.at[0], first, 1)
            push(8, block(2, 0, 1), half2.at[1], first, -1)

        def s5():
            landed(8, half2)
            add_to(block(1, 0, 0), half2.at[0])
            push(9, block(1, 0), full2.at[0], first, 1)
            add_to(block(-1, 0, 1), half2.at[1])
            push(9, block(-1, 0), full2.at[1], first, -1)

        def s6():
            landed(9, full2)
            value = block(0, 0)[...].astype(f32) + full2[0].astype(f32) + full2[1].astype(f32)
            square[w, pl.ds(128 * h, 128), :] = value.astype(bf).reshape(128, 256)

        return [s1(0), s1(1), s1(2), s1(3)], [
            s2(0), s2(1), s2(2), s2(3), s3(0), s4, s3(1), s3(2), s5, s3(3), s6]

    def output(u, final):
        def push(group, src, dst, target):
            remote(src, dst, out_send.at[u, group], out_recv.at[u, group], target).start()

        def landed(group, ref):
            remote(ref, ref, out_send.at[u, group], out_recv.at[u, group], sibling).wait_recv()

        ahead, behind = {"enc": enc_at(1)}, {"enc": enc_at(-1)}
        top, bottom = pl.ds(0, 128), pl.ds(128, 128)

        def block(by, part=None):
            if part is None:
                return outs.at[u, core, around(y, by)]
            return outs.at[u, core, around(y, by), (top, bottom)[part]]

        def p0():
            push(0, outs.at[u, 1 - core], pair_got.at[u], sibling)

        def p1():
            landed(0, pair_got.at[u])
            add_to(block(2), pair_got.at[u, around(y, 2)])
            push(1, block(2, 0), ring_half.at[u, 0], ahead)
            push(1, block(2, 1), ring_half.at[u, 1], behind)
            for by in (1, -1, 0):
                add_to(block(by), pair_got.at[u, around(y, by)])

        def p2():
            landed(1, ring_half.at[u])
            add_to(block(1, 0), ring_half.at[u, 0])
            push(2, block(1), ring_full.at[u, 0], ahead)
            add_to(block(-1, 1), ring_half.at[u, 1])
            push(2, block(-1), ring_full.at[u, 1], behind)

        def p3():
            landed(2, ring_full.at[u])
            value = (block(0)[...].astype(jnp.float32) + ring_full[u, 0].astype(jnp.float32)
                     + ring_full[u, 1].astype(jnp.float32))
            final[...] = value.astype(jnp.bfloat16)

        return [p0, p1, p2, p3]

    outs0, outs1 = output(0, wide.at[0]), output(1, wide.at[1])
    lists = {w: (sum_tree(w, 0), sum_tree(w, 1)) for w in (3, 2, 1, 0)}

    def begin(w):
        for k in range(4):
            lists[w][0][0][k]()
            lists[w][1][0][k]()

    def then(w, lo, hi):
        for k in range(lo, hi):
            lists[w][0][1][k]()
            lists[w][1][1][k]()

    for w in range(4):
        tree_sent(w)
    for u in range(UNITS - STAGES, UNITS):
        staged_sent(u)
    remote(got.at[:, pl.ds(0, 2)], got.at[:, pl.ds(0, 2)], pair_send, pair_recv.at[0], sibling).wait_send()
    for copy in swaps + backs:
        copy.wait_send()
    fill_flat(0, small.at[2], cot, 0, 7)
    begin(3)
    fill_flat(0, small.at[2], cot, 7, 16)
    fill_out(0, small.at[0], 3, False)
    outs0[0]()
    backward()
    fill_flat(1, small.at[3], tok, 0, 7)
    begin(0)
    then(3, 0, 2)
    fill_flat(1, small.at[3], tok, 7, 16)
    then(3, 2, 4)
    backward_rows()
    order_rows()
    fill_rows(0, dvt, 0, 7)
    begin(2)
    then(0, 0, 2)
    fill_rows(0, dvt, 7, 16)
    then(0, 2, 4)
    fill_rows(1, dkt, 0, 7)
    begin(1)
    then(3, 4, 6)
    fill_rows(1, dkt, 7, 16)
    then(2, 0, 2)
    outs0[1]()
    then(2, 2, 4)
    then(3, 6, 8)
    fill_out(1, small.at[1], 2, True)
    outs1[0]()
    outs0[2]()
    then(0, 4, 8)
    then(1, 0, 4)
    outs1[1]()
    then(3, 8, 10)
    outs0[3]()
    then(2, 4, 8)
    outs1[2]()
    then(0, 8, 10)
    then(1, 4, 8)
    then(2, 8, 10)
    then(3, 10, 11)
    then(1, 8, 9)
    then(0, 10, 11)
    then(1, 9, 10)
    outs1[3]()
    then(2, 10, 11)
    then(1, 10, 11)
    for t in range(TREES):
        ref = weights.at[3, pl.ds(0, 15), pl.ds(0, 128)]
        remote(ref, ref, sum_send.at[t], sum_recv.at[t, 0], sibling).wait_send()
    for u in (0, 1):
        for group, ref in enumerate((pair_got.at[u], ring_half.at[u], ring_full.at[u])):
            remote(ref, ref, out_send.at[u, group], out_recv.at[u, group], sibling).wait_send()


def layer(holder, rows, store, wk, wv, wq, wo, tokens, cotangent):
    bf = jnp.bfloat16
    dma = pltpu.SemaphoreType.DMA
    vm = pltpu.VMEM
    return pl.pallas_call(
        layer_kernel,
        out_shape=(jax.ShapeDtypeStruct((2, 256, 512), bf), jax.ShapeDtypeStruct((4, 256, 256), bf)),
        in_specs=[SMEM, SMEM] + [ANY] * 7,
        out_specs=(VMEM, VMEM),
        scratch_shapes=[
            vm((8, 128, 4096), bf),
            vm((2 * CAP, 2, 16, 4096), bf),
            vm((2 * CAP, 2, 16, 4096), bf),
            vm((2, 2 * CAP, 2, 16, 4096), bf),
            vm((UNITS, 4, 16, 4096), bf),
            vm((STAGES, 2, 16, 4096), bf),
            vm((4, 16, 256, 256), bf),
            vm((256, 4096), bf),
            vm((256, 4096), bf),
            vm((2, 2 * CAP, 2, 16, 256), bf),
            vm((2, 2 * CAP, 2, 16, 256), bf),
            vm((UNITS, 4, 16, 256), bf),
            vm((2, 2 * CAP, 2, 16, 256), bf),
            vm((2, 2 * CAP, 2, 16, 256), bf),
            vm((UNITS, 4, 16, 256), bf),
            vm((256, 256), bf),
            vm((4, 256, 256), bf),
            vm((4, 256, 256), bf),
            vm((256, 256), bf),
            vm((4, 2, 64, 256), jnp.float32),
            vm((8, 64, 256), bf),
            vm((4, 256, 256), bf),
            vm((256, 1024), bf),
            vm((256, 1024), bf),
            vm((2, 2, 4, 256, 512), bf),
            vm((4, 4, 2, 64, 256), bf),
            vm((4, 4, 2, 128, 256), bf),
            vm((4, 4, 2, 4, 16, 256), bf),
            vm((4, 4, 2, 2, 4, 16, 256), bf),
            vm((4, 2, 64, 256), bf),
            vm((4, 2, 128, 256), bf),
            vm((4, 2, 4, 16, 256), bf),
            vm((4, 2, 2, 4, 16, 256), bf),
            vm((2, 4, 256, 512), bf),
            vm((2, 2, 128, 512), bf),
            vm((2, 2, 256, 512), bf),
            dma((7,)),
            dma((4,)),
            dma((4, TREE_SEMS)),
            dma((STAGES,)),
            dma((UNITS,)),
            dma(()),
            dma((5,)),
            dma((4,)),
            dma((4,)),
            dma((TREES,)),
            dma((TREES, SUM_SEMS)),
            dma((2, 3)),
            dma((2, 3)),
        ],
        compiler_params=pltpu.CompilerParams(
            collective_id=0, has_side_effects=True, vmem_limit_bytes=62 * 1024 * 1024),
        name="layer",
    )(holder, rows, store, wk, wv, wq, wo, tokens, cotangent)


def finish_kernel(wide, square, cca, gtok, gq, gk, gv, go_out, wide_held, square_held, flipped, load_sem, save_sem):
    parts = [(square.at[i], square_held.at[i], flipped.at[i], out) for i, out in enumerate((gq, gk, gv))]
    parts += [(square.at[3], square_held.at[3], None, go_out)]
    parts += [(wide.at[i], wide_held.at[i], None, out) for i, out in enumerate((cca, gtok))]
    loads = [pltpu.make_async_copy(src, held, load_sem.at[i]) for i, (src, held, _, _) in enumerate(parts)]
    for copy in loads:
        copy.start()
    saves = []
    for i, (_, held, turned, out) in enumerate(parts):
        loads[i].wait()
        if turned is not None:
            turned[...] = held[...].astype(jnp.float32).T.astype(jnp.bfloat16)
        save = pltpu.make_async_copy(held if turned is None else turned, out, save_sem.at[i])
        save.start()
        saves.append(save)
    for copy in saves:
        copy.wait()


def finish(wide, square):
    bf = jnp.bfloat16
    return pl.pallas_call(
        finish_kernel,
        out_shape=(jax.ShapeDtypeStruct((256, 512), bf),) * 2 + (jax.ShapeDtypeStruct((256, 256), bf),) * 4,
        in_specs=[ANY] * 2,
        out_specs=(ANY,) * 6,
        scratch_shapes=[pltpu.VMEM((2, 256, 512), bf), pltpu.VMEM((4, 256, 256), bf), pltpu.VMEM((3, 256, 256), bf),
                        pltpu.SemaphoreType.DMA((6,)), pltpu.SemaphoreType.DMA((6,))],
        name="finish",
    )(wide, square)


def body(tokens, store, holder, rows, wq, wk, wv, wo, cotangent):
    return finish(*layer(holder.reshape(8), rows, store, wk, wv, wq, wo, tokens, cotangent))


def solution(mesh):
    placed = (
        P("dp", None), P(("dp", "enc"), None, None), P("dp", None), P("dp"),
        P("dp", "enc"), P("dp", "enc"), P("dp", "enc"), P("enc", "dp"), P("dp", None),
    )
    return jax.shard_map(
        body, mesh=mesh, in_specs=placed,
        out_specs=(P("dp", "enc"),) * 5 + (P("enc", "dp"),),
        check_vma=False,
    )
```
